256 devices in a mesh: clus: 32 (over x, y, core), rhs: 8 (over z).
Axes of the slice: x: 4, y: 4, z: 8, core: 2. Of those that a mesh axis runs over, the one named last changes fastest.
Arguments:
- leaf_skel: bfloat16 [2048, 256, 64], P('clus', 'rhs'), may hold values from -6 to 6
- transfer: bfloat16 [3968, 64, 64], P('clus'), may hold values from -0.5 to 0.5
- tiles: bfloat16 [4032, 8, 64, 64], P('clus'), may hold values from -0.25 to 0.25
- cols: int32 [4032, 8], P('clus'), may hold values from -1 to 4031, as said below
Outputs:
- leaf_local: float32 [2048, 256, 64], P('clus', 'rhs')
The draws below stay inside these ranges and needn't reach their ends.
Inputs may be any that keep to these rules, and one draw needn't show every extreme that they name: `cols`: every entry is -1 or the index of a node of the same level as its row node whose owning index along clus, the index // 126, differs from the row node's by at most 3.
All inputs are finite; a program needn't handle non-finite values.
Results may differ from the reference program's by a relative error of at most 0.0052.
Values may be sent and summed in bfloat16 or wider, within the bound.
No kernel may reach another device: no remote copies, remote signals or barrier semaphores. Data moves between devices by JAX's collectives and lax.ppermute only.
A program may use at most 128 MiB of HBM per device.

```python
import jax
import jax.numpy as jnp
from jax import lax

K = 64
BLK = 2
LEV = 6
REACH = 3
P_SIZE = 8
RHS = 256
LEAF_DEV = 64
NODES_DEV = 126
NLEAF = 2048
NTOT = 4032
N_CLUS = 32


def draw_cols(key, part):
    key = jax.random.fold_in(key, 7)
    first_key, second_key, third_key = jax.random.split(key, 3)
    total_nodes = N_CLUS * NODES_DEV
    node_ids = jnp.arange(total_nodes, dtype=jnp.int32)
    owner = node_ids // NODES_DEV
    local_row = node_ids % NODES_DEV
    level_id = jnp.zeros((total_nodes,), jnp.int32)
    for step_id in range(1, LEV):
        level_id = level_id + (local_row >= BLK * (2 ** step_id - 1)).astype(jnp.int32)
    powers = jnp.left_shift(jnp.ones((total_nodes,), jnp.int32), level_id)
    level_offset = BLK * (powers - 1)
    level_count = BLK * powers
    moved = jax.random.randint(first_key, (total_nodes, P_SIZE), -REACH, REACH + 1)
    picked = jax.random.randint(second_key, (total_nodes, P_SIZE), 0, 2 ** 30) % level_count[:, None]
    live_slot = jax.random.randint(third_key, (total_nodes, P_SIZE), 0, 5) > 0
    target = owner[:, None] + moved
    usable = live_slot & (target >= 0) & (target < N_CLUS)
    column = target * NODES_DEV + level_offset[:, None] + picked
    result = jnp.where(usable, column, -1).astype(jnp.int32)
    result = result.at[total_nodes - 2, 0].set(jnp.int32(total_nodes - 1))
    result = result.at[0, P_SIZE - 1].set(jnp.int32(-1))
    return result


def level_of(key, shape, pieces, least, largest):
    loudness, own = 1.0, jax.random.fold_in(key, 6)
    for position, parts in pieces:
        steps = jnp.exp(jax.random.uniform(jax.random.fold_in(own, position), (parts,), jnp.float32, least / len(pieces), largest / len(pieces)))
        loudness = loudness * jnp.repeat(steps, shape[position] // parts).reshape([-1 if axis == position else 1 for axis in range(len(shape))])
    return loudness


def gaussian(rng, extent, scale, bound, pieces=(), kind=jnp.bfloat16):
    level = level_of(rng, extent, pieces, -0.22, 0.18) if pieces else 1.0
    array = jax.random.normal(rng, extent, jnp.float32) * scale * level
    return jnp.minimum(jnp.maximum(array, -bound), bound).astype(kind)


def setup_inputs(seed: int = 0) -> dict:
    arg_keys = jax.random.split(jax.random.key(seed), 5)
    return {
        "leaf_skel": gaussian(arg_keys[0], (NLEAF, RHS, K), 1.0, 6.0, ((0, 32), (1, 8))),
        "transfer": gaussian(arg_keys[1], (NTOT - BLK * N_CLUS, K, K), (2 * K) ** -0.5, 0.5, ((0, 32),)),
        "tiles": gaussian(arg_keys[2], (NTOT, P_SIZE, K, K), (P_SIZE * K) ** -0.5, 0.25, ((0, 32),)),
        "cols": draw_cols(jax.random.fold_in(arg_keys[4], 71), 0),
    }


def reference(leaf_skel, transfer, tiles, cols):
    highest = lax.Precision.HIGHEST
    skeletons = [None] * LEV
    skeletons[LEV - 1] = leaf_skel.reshape(N_CLUS, LEAF_DEV, RHS, K)
    basis = transfer.reshape(N_CLUS, NODES_DEV - BLK, K, K)
    for level_id in range(LEV - 2, -1, -1):
        cluster_count = BLK * 2 ** level_id
        first_row = BLK * (2 ** (level_id + 1) - 1) - BLK
        children = skeletons[level_id + 1].reshape(N_CLUS, cluster_count, 2, RHS, K).astype(jnp.float32)
        coeffs = basis[:, first_row:first_row + 2 * cluster_count].reshape(N_CLUS, cluster_count, 2, K, K).astype(jnp.float32)
        parent = jnp.einsum("ncjrk,ncjkq->ncrq", children, coeffs, precision=highest)
        skeletons[level_id] = parent.astype(jnp.bfloat16)
    packed = jnp.concatenate(skeletons, axis=1).reshape(NTOT, RHS, K)
    coupled = jnp.zeros((NTOT, RHS, K), jnp.float32)
    for slot_id in range(P_SIZE):
        column = cols[:, slot_id]
        live_slot = column >= 0
        fetched = packed[jnp.maximum(column, 0)].astype(jnp.float32)
        term = jnp.einsum("grk,gkq->grq", fetched, tiles[:, slot_id].astype(jnp.float32), precision=highest)
        coupled = coupled + jnp.where(live_slot[:, None, None], term, jnp.float32(0.0))
    coupled = coupled.reshape(N_CLUS, NODES_DEV, RHS, K)
    local_coef = coupled[:, 0:BLK]
    for level_id in range(1, LEV):
        cluster_count = BLK * 2 ** level_id
        first_row = BLK * (2 ** level_id - 1)
        coeffs = basis[:, first_row - BLK:first_row - BLK + cluster_count].reshape(N_CLUS, cluster_count // 2, 2, K, K).astype(jnp.float32)
        downward = jnp.einsum("ncrk,ncjqk->ncjrq", local_coef, coeffs, precision=highest)
        downward = downward.reshape(N_CLUS, cluster_count, RHS, K)
        local_coef = coupled[:, first_row:first_row + cluster_count] + downward
    return local_coef.reshape(NLEAF, RHS, K)
```

```python
import functools

import jax
import jax.numpy as jnp
from jax import lax
from jax.experimental import pallas as pl
from jax.experimental.pallas import tpu as pltpu
from jax.sharding import PartitionSpec as P

LEV = 6
REACH = 3
SLOTS = 8
K = 64
LANES = 128
LEAF_PAIRS = 32
UPPER_PAIRS = 31
NODES = 126
ROWS = 32
MIB = 2**20
BF16 = jnp.bfloat16
F32 = jnp.float32
WHOLE = pl.BlockSpec(memory_space=pltpu.VMEM)
IN_HBM = pl.BlockSpec(memory_space=pl.ANY)
IN_SMEM = pl.BlockSpec(memory_space=pltpu.SMEM)


def pair_offset(level):
    return 2**level - 1


def params(mib):
    return pltpu.CompilerParams(vmem_limit_bytes=mib * MIB)


def pack_kernel(leaf_ref, out_ref):
    for j in range(LEAF_PAIRS):
        out_ref[j] = jnp.concatenate([leaf_ref[2 * j], leaf_ref[2 * j + 1]], axis=1)


def pack_leaves(leaf):
    return pl.pallas_call(
        pack_kernel,
        in_specs=[WHOLE],
        out_specs=WHOLE,
        out_shape=jax.ShapeDtypeStruct((LEAF_PAIRS, ROWS, LANES), BF16),
        compiler_params=params(8),
    )(leaf)


E_STRIDE = K + 1
E_NODES = NODES - 2


def upward_kernel(coeff_ref, leaf_ref, basis_ref, skel_ref, stage):
    node = lax.broadcasted_iota(jnp.int32, (E_NODES, LANES), 0)
    lane = lax.broadcasted_iota(jnp.int32, (E_NODES, LANES), 1)
    own = ((node // 2) % 2) == (lane // K)
    for a in range(K):
        slab = coeff_ref[a].astype(F32)
        twice = jnp.concatenate([slab, slab], axis=0).T
        stage[pl.ds(a, E_NODES, stride=E_STRIDE), :] = jnp.where(own, twice, 0.0)
    for g in range(E_NODES):
        basis_ref[g // 4, (g % 4) * K : (g % 4 + 1) * K, :] = stage[pl.ds(g * E_STRIDE, K), :].astype(BF16)
    for level in range(LEV - 2, -1, -1):
        first = pair_offset(level)
        below = pair_offset(level + 1)
        for i in range(2**level):
            if level == LEV - 2:
                left, right = leaf_ref[2 * i], leaf_ref[2 * i + 1]
            else:
                left, right = skel_ref[below + 2 * i], skel_ref[below + 2 * i + 1]
            children = jnp.concatenate([left, right], axis=1)
            parent = jnp.dot(children, basis_ref[first + i], preferred_element_type=F32)
            skel_ref[first + i] = parent.astype(BF16)


def upward(coeffs, leaf_pairs):
    return pl.pallas_call(
        upward_kernel,
        in_specs=[WHOLE, WHOLE],
        out_specs=(WHOLE, WHOLE),
        out_shape=(
            pltpu.VMEM((UPPER_PAIRS, 4 * K, LANES), BF16),
            jax.ShapeDtypeStruct((UPPER_PAIRS, ROWS, LANES), BF16),
        ),
        scratch_shapes=[pltpu.VMEM((E_NODES * E_STRIDE + 8, LANES), F32)],
        compiler_params=params(14),
    )(coeffs, leaf_pairs)


DEPTH = 16
CHUNKS = 4 * K // DEPTH
STRIDE = DEPTH + 1


def weights_kernel(tiles_ref, out_ref, held, stage, sem):
    per_slot = K // DEPTH

    def copy(i):
        slot, part = i // per_slot, pl.ds(i % per_slot * DEPTH, DEPTH)
        return pltpu.make_async_copy(tiles_ref.at[:, slot, part], held.at[:, slot, part], sem.at[i])

    for i in range(CHUNKS):
        copy(i).start()

    def step(i, carry):
        copy(i).wait()
        slot, base = i // per_slot, i % per_slot * DEPTH
        for k in range(DEPTH):
            slab = held[:, slot, base + k].reshape(LANES, NODES).astype(F32)
            stage[pl.ds(k, NODES, stride=STRIDE), :] = slab.T
        rows = pl.ds(pl.multiple_of(i * DEPTH, DEPTH), DEPTH)
        for g in range(NODES):
            out_ref[g, rows, :] = stage[pl.ds(g * STRIDE, DEPTH), :].astype(BF16)
        return carry

    lax.fori_loop(0, CHUNKS, step, 0)


def coupling_weights(tiles):
    slabs = jnp.transpose(tiles, (1, 2, 3, 0)).reshape(2, SLOTS // 2, K, K, NODES)
    return pl.pallas_call(
        weights_kernel,
        in_specs=[IN_HBM],
        out_specs=WHOLE,
        out_shape=pltpu.VMEM((NODES, 4 * K, LANES), BF16),
        scratch_shapes=[
            pltpu.VMEM((2, SLOTS // 2, K, K, NODES), BF16),
            pltpu.VMEM((NODES * STRIDE + 8, LANES), F32),
            pltpu.SemaphoreType.DMA((CHUNKS,)),
        ],
        compiler_params=params(22),
        cost_estimate=pl.CostEstimate(flops=0, bytes_accessed=30 * MIB, transcendentals=0),
    )(slabs)


def swap_halves(pair):
    return pltpu.roll(pair, K, 1)


def fill_table(blocks, table, pairs):
    count = 7 * pairs
    for b, block in enumerate(blocks):
        def one(i, carry):
            pair = block[i]
            table[0, b * pairs + i] = pair
            table[1, b * pairs + i] = swap_halves(pair.astype(F32)).astype(BF16)
            return carry

        lax.fori_loop(0, pairs, one, 0, unroll=4)
    for half in range(2):
        table[half, count] = jnp.zeros((ROWS, LANES), BF16)


def couple_pair(j, first_node, place_ref, table, weights_ref):
    lane = lax.broadcasted_iota(jnp.int32, (ROWS, LANES), 1)
    low = lane < K

    def fetch(slot, node):
        place = place_ref[slot, node]
        return table[place >> 12, place & 4095]

    products = []
    for side in range(2):
        node = first_node + 2 * j + side
        halves = []
        for half in range(2):
            quarter = []
            for duo in range(2):
                slot = half * 4 + duo * 2
                quarter.append(jnp.where(low, fetch(slot, node), fetch(slot + 1, node)))
            halves.append(jnp.concatenate(quarter, axis=1))
        operand = jnp.concatenate(halves, axis=0)
        products.append(jnp.dot(operand, weights_ref[node], preferred_element_type=F32))
    even, odd = products
    straight = jnp.where(low, even[:ROWS], odd[ROWS:])
    crossed = jnp.where(low, odd[:ROWS], even[ROWS:])
    return straight + swap_halves(crossed)


def upper_kernel(place_ref, *refs):
    blocks, (weights_ref, basis_ref, out_ref, table, local) = refs[:7], refs[7:]
    fill_table(blocks, table, UPPER_PAIRS)

    def one(j, carry):
        local[j] = couple_pair(j, 0, place_ref, table, weights_ref)
        return carry

    lax.fori_loop(0, UPPER_PAIRS, one, 0)
    contract = (((1,), (1,)), ((), ()))
    for level in range(LEV - 1):
        first = pair_offset(level)
        below = pair_offset(level + 1)
        for i in range(2**level):
            parent = local[first + i].astype(BF16)
            children = lax.dot_general(parent, basis_ref[first + i], contract, preferred_element_type=F32)
            for side in range(2):
                part = children[:, side * LANES : (side + 1) * LANES]
                if level == LEV - 2:
                    out_ref[2 * i + side] = part
                else:
                    local[below + 2 * i + side] += part


def upper_levels(place, blocks, weights, basis):
    return pl.pallas_call(
        upper_kernel,
        in_specs=[IN_SMEM] + [WHOLE] * 9,
        out_specs=WHOLE,
        out_shape=jax.ShapeDtypeStruct((LEAF_PAIRS, ROWS, LANES), F32),
        scratch_shapes=[
            pltpu.VMEM((2, 7 * UPPER_PAIRS + 1, ROWS, LANES), BF16),
            pltpu.VMEM((UPPER_PAIRS, ROWS, LANES), F32),
        ],
        compiler_params=params(24),
    )(place, *blocks, weights, basis)


def leaf_kernel(place_ref, *refs):
    blocks, (weights_ref, down_ref, out_ref, table) = refs[:7], refs[7:]
    fill_table(blocks, table, LEAF_PAIRS)

    def one(j, carry):
        pair = couple_pair(j, 2 * UPPER_PAIRS, place_ref, table, weights_ref) + down_ref[j]
        out_ref[2 * j] = pair[:, :K]
        out_ref[2 * j + 1] = swap_halves(pair)[:, :K]
        return carry

    lax.fori_loop(0, LEAF_PAIRS, one, 0)


def leaf_level(place, blocks, weights, down):
    return pl.pallas_call(
        leaf_kernel,
        in_specs=[IN_SMEM] + [WHOLE] * 9,
        out_specs=WHOLE,
        out_shape=jax.ShapeDtypeStruct((2 * LEAF_PAIRS, ROWS, K), F32),
        scratch_shapes=[pltpu.VMEM((2, 7 * LEAF_PAIRS + 1, ROWS, LANES), BF16)],
        compiler_params=params(24),
    )(place, *blocks, weights, down)


def places(cols, own_index):
    column = cols.T
    owner = column // NODES
    row = column - owner * NODES
    away = owner - own_index
    away = jnp.where(own_index % 2 == 0, away, -away) + REACH
    slot = lax.broadcasted_iota(jnp.int32, column.shape, 0)
    node = lax.broadcasted_iota(jnp.int32, column.shape, 1)
    is_leaf = node >= 2 * UPPER_PAIRS
    pairs = jnp.where(is_leaf, LEAF_PAIRS, UPPER_PAIRS)
    pair = jnp.where(is_leaf, row // 2 - UPPER_PAIRS, row // 2)
    swapped = (row + slot) % 2
    return jnp.where(column >= 0, away * pairs + pair + 4096 * swapped, 7 * pairs)


def shards(leaf_skel, transfer, tiles, cols):
    count = lax.axis_size("clus")
    own_index = lax.axis_index("clus")

    def moved(block, target):
        return lax.ppermute(block, "clus", [(i, target(i) % count) for i in range(count)])

    def other_core(i):
        return i ^ 1

    def outward(i):
        return i + 2 if i % 2 == 0 else i - 2

    def across(i):
        return i + 1 if i % 2 == 1 else i - 1

    place = places(cols, own_index)
    leaf = pack_leaves(leaf_skel)

    def exchange(own):
        near = moved(own, across)
        next_near = moved(own, outward)
        partner = moved(own, other_core)
        far = moved(near, outward)
        return own, near, next_near, partner, far

    def finish(own, near, next_near, partner, far):
        both = moved(jnp.concatenate([next_near, near], axis=0), other_core)
        size = own.shape[0]
        return (far, next_near, near, own, partner, both[size:], both[:size])

    leaf_parts = exchange(leaf)
    basis, upper = upward(jnp.transpose(transfer, (1, 2, 0)), leaf)
    upper_parts = exchange(upper)
    weights = coupling_weights(tiles)
    down = upper_levels(place, finish(*upper_parts), weights, basis)
    return leaf_level(place, finish(*leaf_parts), weights, down)


def solution(mesh):
    in_specs = (
        P("clus", "rhs", None),
        P("clus", None, None),
        P("clus", None, None, None),
        P("clus", None),
    )
    out_specs = P("clus", "rhs", None)
    return jax.shard_map(shards, mesh=mesh, in_specs=in_specs, out_specs=out_specs, check_vma=False)
```

```python
import functools

import jax
import jax.numpy as jnp
from jax import lax
from jax.experimental import pallas as pl
from jax.experimental.pallas import tpu as pltpu
from jax.sharding import PartitionSpec as P

LEV = 6
REACH = 3
SLOTS = 8
K = 64
LANES = 128
LEAF_PAIRS = 32
UPPER_PAIRS = 31
PAIRS = LEAF_PAIRS + UPPER_PAIRS
NODES = 126
ROWS = 32
MIB = 2**20
BF16 = jnp.bfloat16
F32 = jnp.float32
WHOLE = pl.BlockSpec(memory_space=pltpu.VMEM)
IN_HBM = pl.BlockSpec(memory_space=pltpu.HBM)
IN_SMEM = pl.BlockSpec(memory_space=pltpu.SMEM)


def pair_offset(level):
    return 2**level - 1


def params(mib):
    return pltpu.CompilerParams(vmem_limit_bytes=mib * MIB)


def each(count, width, body):
    def several(i, carry):
        for u in range(width):
            body(i * width + u)
        return carry

    lax.fori_loop(0, count // width, several, 0)
    for i in range(count // width * width, count):
        body(i)


def front_kernel(leaf_ref, coeff_ref, out_ref, held_ref, leaf, sems):
    first = pltpu.make_async_copy(leaf_ref, leaf, sems.at[0])
    second = pltpu.make_async_copy(coeff_ref, held_ref, sems.at[1])
    first.start()
    second.start()
    first.wait()
    for j in range(LEAF_PAIRS):
        out_ref[j] = jnp.concatenate([leaf[2 * j], leaf[2 * j + 1]], axis=1)
    second.wait()


def front(leaf, coeffs):
    return pl.pallas_call(
        front_kernel,
        in_specs=[IN_HBM, IN_HBM],
        out_specs=(WHOLE, WHOLE),
        out_shape=(pltpu.VMEM((LEAF_PAIRS, ROWS, LANES), BF16), pltpu.VMEM(coeffs.shape, BF16)),
        scratch_shapes=[pltpu.VMEM(leaf.shape, BF16), pltpu.SemaphoreType.DMA((2,))],
        compiler_params=params(60),
    )(leaf, coeffs)


E_STRIDE = K + 1
E_NODES = NODES - 2


def upward_kernel(coeff_ref, leaf_ref, basis_ref, skel_ref, stage):
    node = lax.broadcasted_iota(jnp.int32, (E_NODES, LANES), 0)
    lane = lax.broadcasted_iota(jnp.int32, (E_NODES, LANES), 1)
    own = ((node // 2) % 2) == (lane // K)
    for a in range(K):
        slab = coeff_ref[a].astype(F32)
        twice = jnp.concatenate([slab, slab], axis=0).T
        stage[pl.ds(a, E_NODES, stride=E_STRIDE), :] = jnp.where(own, twice, 0.0)
    for g in range(E_NODES):
        basis_ref[g // 4, (g % 4) * K : (g % 4 + 1) * K, :] = stage[pl.ds(g * E_STRIDE, K), :].astype(BF16)
    for level in range(LEV - 2, -1, -1):
        first = pair_offset(level)
        below = pair_offset(level + 1)
        for i in range(2**level):
            if level == LEV - 2:
                left, right = leaf_ref[2 * i], leaf_ref[2 * i + 1]
            else:
                left, right = skel_ref[below + 2 * i], skel_ref[below + 2 * i + 1]
            children = jnp.concatenate([left, right], axis=1)
            parent = jnp.dot(children, basis_ref[first + i], preferred_element_type=F32)
            skel_ref[first + i] = parent.astype(BF16)


def upward(coeffs, leaf_pairs):
    return pl.pallas_call(
        upward_kernel,
        in_specs=[WHOLE, WHOLE],
        out_specs=(WHOLE, WHOLE),
        out_shape=(
            pltpu.VMEM((UPPER_PAIRS, 4 * K, LANES), BF16),
            pltpu.VMEM((UPPER_PAIRS, ROWS, LANES), BF16),
        ),
        scratch_shapes=[pltpu.VMEM((E_NODES * E_STRIDE + 8, LANES), F32)],
        compiler_params=params(14),
    )(coeffs, leaf_pairs)


DEPTH = 16
CHUNKS = 2 * K // DEPTH
STRIDE = DEPTH + 1
DUOS = SLOTS // 4


def places(cols_ref, device_ref, place_ref):
    device = device_ref[0]
    column = cols_ref[...]
    slot = lax.broadcasted_iota(jnp.int32, column.shape, 0)
    is_leaf = lax.broadcasted_iota(jnp.int32, column.shape, 1) >= 2 * UPPER_PAIRS
    past = column - (device - REACH) * NODES
    block = jnp.zeros(column.shape, jnp.int32)
    for step in range(1, 2 * REACH + 1):
        block += jnp.where(past >= step * NODES, 1, 0)
    row = past - block * NODES
    block = jnp.where((device & 1) == 0, block, 2 * REACH - block)
    pairs = jnp.where(is_leaf, LEAF_PAIRS, UPPER_PAIRS)
    pair = (row >> 1) - jnp.where(is_leaf, UPPER_PAIRS, 0)
    swapped = (row + slot) & 1
    place_ref[...] = jnp.where(column >= 0, block * pairs + pair + 4096 * swapped, 7 * pairs)


def transpose_tiles(duo, tiles_ref, out_ref, held, stage, sem, beside):
    per_slot = K // DEPTH

    def copy(i):
        slot, part = i // per_slot, pl.ds(i % per_slot * DEPTH, DEPTH)
        return pltpu.make_async_copy(tiles_ref.at[:, 2 * duo + slot, part], held.at[:, slot, part], sem.at[i])

    for i in range(CHUNKS):
        copy(i).start()
    beside()

    def step(i, carry):
        copy(i).wait()
        slot, base = i // per_slot, i % per_slot * DEPTH
        for k in range(DEPTH):
            slab = held[:, slot, base + k].reshape(LANES, NODES).astype(F32)
            stage[pl.ds(k, NODES, stride=STRIDE), :] = slab.T
        rows = pl.ds(pl.multiple_of(i * DEPTH, DEPTH), DEPTH)
        for g in range(NODES):
            out_ref[g, rows, :] = stage[pl.ds(g * STRIDE, DEPTH), :].astype(BF16)
        return carry

    lax.fori_loop(0, CHUNKS, step, 0)


TRANSPOSE_SCRATCH = [
    pltpu.VMEM((2, 2, K, K, NODES), BF16),
    pltpu.VMEM((NODES * STRIDE + 8, LANES), F32),
    pltpu.SemaphoreType.DMA((CHUNKS,)),
]


def first_weights_kernel(tiles_ref, cols_ref, device_ref, out_ref, place_ref, held, stage, sem):
    transpose_tiles(0, tiles_ref, out_ref, held, stage, sem, lambda: places(cols_ref, device_ref, place_ref))


def first_weights(slabs, cols, device):
    return pl.pallas_call(
        first_weights_kernel,
        in_specs=[IN_HBM, WHOLE, IN_SMEM],
        out_specs=(WHOLE, WHOLE),
        out_shape=(
            pltpu.VMEM((NODES, 2 * K, LANES), BF16),
            jax.ShapeDtypeStruct((SLOTS, NODES), jnp.int32),
        ),
        scratch_shapes=TRANSPOSE_SCRATCH,
        compiler_params=params(46),
    )(slabs, cols.T, device)


def swap_halves(pair):
    return pltpu.roll(pair, K, 1)


def fill_block(table, block, number, pairs, first=0):
    for i in range(pairs):
        pair = block[first + i]
        table[0, number * pairs + i] = pair
        table[1, number * pairs + i] = swap_halves(pair)


def fill_first(own_ref, near_ref, next_ref, table_ref, sent_ref, pairs):
    for place, (number, block) in enumerate(((REACH, own_ref), (REACH - 1, near_ref), (REACH - 2, next_ref))):
        fill_block(table_ref, block, number, pairs)
        for i in range(pairs):
            sent_ref[place * pairs + i] = block[i]
    for half in range(2):
        table_ref[half, 7 * pairs] = jnp.zeros((ROWS, LANES), BF16)


def table_and_sent(pairs):
    return (
        pltpu.VMEM((2, 7 * pairs + 1, ROWS, LANES), BF16),
        pltpu.VMEM((3 * pairs, ROWS, LANES), BF16),
    )


def second_weights_kernel(tiles_ref, own_ref, near_ref, next_ref, out_ref, table_ref, sent_ref, held, stage, sem):
    def beside():
        fill_first(own_ref, near_ref, next_ref, table_ref, sent_ref, LEAF_PAIRS)

    transpose_tiles(1, tiles_ref, out_ref, held, stage, sem, beside)


def second_weights(slabs, own, near, next_near):
    return pl.pallas_call(
        second_weights_kernel,
        in_specs=[IN_HBM, WHOLE, WHOLE, WHOLE],
        out_specs=(WHOLE, WHOLE, WHOLE),
        out_shape=(pltpu.VMEM((NODES, 2 * K, LANES), BF16), *table_and_sent(LEAF_PAIRS)),
        scratch_shapes=TRANSPOSE_SCRATCH,
        compiler_params=params(38),
    )(slabs, own, near, next_near)


def upper_table_kernel(own_ref, near_ref, next_ref, table_ref, sent_ref):
    fill_first(own_ref, near_ref, next_ref, table_ref, sent_ref, UPPER_PAIRS)


def upper_table(own, near, next_near):
    return pl.pallas_call(
        upper_table_kernel,
        in_specs=[WHOLE, WHOLE, WHOLE],
        out_specs=(WHOLE, WHOLE),
        out_shape=table_and_sent(UPPER_PAIRS),
        compiler_params=params(4),
    )(own, near, next_near)


def fill_rest(table, far_ref, other_ref, pairs):
    fill_block(table, far_ref, 0, pairs)
    for step in range(REACH):
        fill_block(table, other_ref, REACH + 1 + step, pairs, step * pairs)


def couple_pair(j, first_node, place_ref, table, weights_refs):
    low = lax.broadcasted_iota(jnp.int32, (ROWS, LANES), 1) < K

    def fetch(slot, node):
        place = place_ref[slot, node]
        return table[place >> 12, place & 4095]

    products = []
    for side in range(2):
        node = first_node + 2 * j + side
        total = None
        for duo in range(DUOS):
            halves = []
            for half in range(2):
                slot = half * 4 + duo * 2
                halves.append(jnp.where(low, fetch(slot, node), fetch(slot + 1, node)))
            operand = jnp.concatenate(halves, axis=0)
            term = jnp.dot(operand, weights_refs[duo][node], preferred_element_type=F32)
            total = term if total is None else total + term
        products.append(total)
    even, odd = products
    straight = jnp.where(low, even[:ROWS], odd[ROWS:])
    crossed = jnp.where(low, odd[:ROWS], even[ROWS:])
    return straight + swap_halves(crossed)


def leaf_kernel(place_ref, far_ref, other_ref, first_ref, second_ref, given_ref, out_ref, table):
    fill_rest(table, far_ref, other_ref, LEAF_PAIRS)

    def one(j):
        out_ref[j] = couple_pair(j, 2 * UPPER_PAIRS, place_ref, table, (first_ref, second_ref))

    each(LEAF_PAIRS, 16, one)


def leaf_level(place, far, other, weights, table):
    return pl.pallas_call(
        leaf_kernel,
        in_specs=[IN_SMEM] + [WHOLE] * 5,
        out_specs=(WHOLE, WHOLE),
        out_shape=(pltpu.VMEM((LEAF_PAIRS, ROWS, LANES), F32), table_and_sent(LEAF_PAIRS)[0]),
        input_output_aliases={5: 1},
        compiler_params=params(4),
    )(place, far, other, *weights, table)[0]


def upper_kernel(place_ref, far_ref, other_ref, first_ref, second_ref, basis_ref, leaf_ref, given_ref, out_ref, table, local):
    fill_rest(table, far_ref, other_ref, UPPER_PAIRS)

    def one(j):
        local[j] = couple_pair(j, 0, place_ref, table, (first_ref, second_ref))

    each(UPPER_PAIRS, 10, one)
    contract = (((1,), (1,)), ((), ()))
    for level in range(LEV - 1):
        first = pair_offset(level)
        below = pair_offset(level + 1)
        for i in range(2**level):
            parent = local[first + i].astype(BF16)
            children = lax.dot_general(parent, basis_ref[first + i], contract, preferred_element_type=F32)
            for side in range(2):
                part = children[:, side * LANES : (side + 1) * LANES]
                if level == LEV - 2:
                    pair = part + leaf_ref[2 * i + side]
                    out_ref[4 * i + 2 * side] = pair[:, :K]
                    out_ref[4 * i + 2 * side + 1] = swap_halves(pair)[:, :K]
                else:
                    local[below + 2 * i + side] += part


def upper_levels(place, far, other, weights, basis, leaf, table):
    return pl.pallas_call(
        upper_kernel,
        in_specs=[IN_SMEM] + [WHOLE] * 7,
        out_specs=(WHOLE, WHOLE),
        out_shape=(
            jax.ShapeDtypeStruct((2 * LEAF_PAIRS, ROWS, K), F32),
            table_and_sent(UPPER_PAIRS)[0],
        ),
        input_output_aliases={7: 1},
        scratch_shapes=[pltpu.VMEM((UPPER_PAIRS, ROWS, LANES), F32)],
        compiler_params=params(6),
    )(place, far, other, *weights, basis, leaf, table)[0]


def shards(leaf_skel, transfer, tiles, cols):
    count = lax.axis_size("clus")
    own_index = lax.axis_index("clus")

    def moved(block, target):
        return lax.ppermute(block, "clus", [(i, target(i) % count) for i in range(count)])

    def other_core(i):
        return i ^ 1

    def outward(i):
        return i + 2 if i % 2 == 0 else i - 2

    def across(i):
        return i + 1 if i % 2 == 1 else i - 1

    slabs = jnp.transpose(tiles, (1, 2, 3, 0)).reshape(2, SLOTS // 2, K, K, NODES)
    leaf, coeffs = front(leaf_skel, jnp.transpose(transfer, (1, 2, 0)))
    near_leaf, next_leaf = moved(leaf, across), moved(leaf, outward)
    basis, upper = upward(coeffs, leaf)
    near_upper, next_upper = moved(upper, across), moved(upper, outward)
    slabs, upper = lax.optimization_barrier((slabs, upper))
    first, place = first_weights(slabs, cols, own_index.astype(jnp.int32).reshape(1))
    near_leaf, next_leaf, place = lax.optimization_barrier((near_leaf, next_leaf, place))
    far_leaf = moved(near_leaf, outward)
    second, leaf_table, sent_leaf = second_weights(slabs, leaf, near_leaf, next_leaf)
    other_leaf = moved(sent_leaf, other_core)
    far_upper = moved(near_upper, outward)
    table, sent_upper = upper_table(upper, near_upper, next_upper)
    other_upper = moved(sent_upper, other_core)
    weights = (first, second)
    leaf_local = leaf_level(place, far_leaf, other_leaf, weights, leaf_table)
    return upper_levels(place, far_upper, other_upper, weights, basis, leaf_local, table)


def solution(mesh):
    in_specs = (
        P("clus", "rhs", None),
        P("clus", None, None),
        P("clus", None, None, None),
        P("clus", None),
    )
    out_specs = P("clus", "rhs", None)
    return jax.shard_map(shards, mesh=mesh, in_specs=in_specs, out_specs=out_specs, check_vma=False)
```

```python
import functools

import jax
import jax.numpy as jnp
from jax import lax
from jax.experimental import pallas as pl
from jax.experimental.pallas import tpu as pltpu
from jax.sharding import PartitionSpec as P

LEV = 6
REACH = 3
SLOTS = 8
K = 64
LANES = 128
LEAF_PAIRS = 32
UPPER_PAIRS = 31
PAIRS = LEAF_PAIRS + UPPER_PAIRS
NODES = 126
ROWS = 32
MIB = 2**20
BF16 = jnp.bfloat16
F32 = jnp.float32
WHOLE = pl.BlockSpec(memory_space=pltpu.VMEM)
IN_HBM = pl.BlockSpec(memory_space=pltpu.HBM)
IN_SMEM = pl.BlockSpec(memory_space=pltpu.SMEM)


def pair_offset(level):
    return 2**level - 1


def in_hbm(array):
    return pltpu.with_memory_space_constraint(array, pltpu.HBM)


def in_vmem(*arrays):
    return tuple(pltpu.with_memory_space_constraint(array, pltpu.VMEM) for array in arrays)


def params(mib):
    return pltpu.CompilerParams(vmem_limit_bytes=mib * MIB)


def each(count, width, body):
    def several(i, carry):
        for u in range(width):
            body(i * width + u)
        return carry

    lax.fori_loop(0, count // width, several, 0)
    for i in range(count // width * width, count):
        body(i)


def front_kernel(leaf_ref, coeff_ref, out_ref, held_ref, leaf, sems):
    first = pltpu.make_async_copy(leaf_ref, leaf, sems.at[0])
    second = pltpu.make_async_copy(coeff_ref, held_ref, sems.at[1])
    first.start()
    second.start()
    first.wait()
    for j in range(LEAF_PAIRS):
        out_ref[j] = jnp.concatenate([leaf[2 * j], leaf[2 * j + 1]], axis=1)
    second.wait()


def front(leaf, coeffs):
    return pl.pallas_call(
        front_kernel,
        in_specs=[IN_HBM, IN_HBM],
        out_specs=(WHOLE, WHOLE),
        out_shape=(pltpu.VMEM((LEAF_PAIRS, ROWS, LANES), BF16), pltpu.VMEM(coeffs.shape, BF16)),
        scratch_shapes=[pltpu.VMEM(leaf.shape, BF16), pltpu.SemaphoreType.DMA((2,))],
        compiler_params=params(8),
    )(in_hbm(leaf), in_hbm(coeffs))


E_STRIDE = K + 1
E_NODES = NODES - 2


def upward_kernel(coeff_ref, leaf_ref, basis_ref, skel_ref, stage):
    node = lax.broadcasted_iota(jnp.int32, (E_NODES, LANES), 0)
    lane = lax.broadcasted_iota(jnp.int32, (E_NODES, LANES), 1)
    own = ((node // 2) % 2) == (lane // K)
    for a in range(K):
        slab = coeff_ref[a].astype(F32)
        twice = jnp.concatenate([slab, slab], axis=0).T
        stage[pl.ds(a, E_NODES, stride=E_STRIDE), :] = jnp.where(own, twice, 0.0)
    for g in range(E_NODES):
        basis_ref[g // 4, (g % 4) * K : (g % 4 + 1) * K, :] = stage[pl.ds(g * E_STRIDE, K), :].astype(BF16)
    for level in range(LEV - 2, -1, -1):
        first = pair_offset(level)
        below = pair_offset(level + 1)
        for i in range(2**level):
            if level == LEV - 2:
                left, right = leaf_ref[2 * i], leaf_ref[2 * i + 1]
            else:
                left, right = skel_ref[below + 2 * i], skel_ref[below + 2 * i + 1]
            children = jnp.concatenate([left, right], axis=1)
            parent = jnp.dot(children, basis_ref[first + i], preferred_element_type=F32)
            skel_ref[first + i] = parent.astype(BF16)


def upward(coeffs, leaf_pairs):
    return pl.pallas_call(
        upward_kernel,
        in_specs=[WHOLE, WHOLE],
        out_specs=(WHOLE, WHOLE),
        out_shape=(
            pltpu.VMEM((UPPER_PAIRS, 4 * K, LANES), BF16),
            pltpu.VMEM((UPPER_PAIRS, ROWS, LANES), BF16),
        ),
        scratch_shapes=[pltpu.VMEM((E_NODES * E_STRIDE + 8, LANES), F32)],
        compiler_params=params(14),
    )(*in_vmem(coeffs, leaf_pairs))


DEPTH = 32
CHUNKS = 2 * K // DEPTH
STRIDE = DEPTH + 1
DUOS = SLOTS // 4


def places(cols_ref, device_ref, place_ref):
    device = device_ref[0]
    column = cols_ref[...]
    slot = lax.broadcasted_iota(jnp.int32, column.shape, 0)
    is_leaf = lax.broadcasted_iota(jnp.int32, column.shape, 1) >= 2 * UPPER_PAIRS
    past = column - (device - REACH) * NODES
    block = jnp.zeros(column.shape, jnp.int32)
    for step in range(1, 2 * REACH + 1):
        block += jnp.where(past >= step * NODES, 1, 0)
    row = past - block * NODES
    block = jnp.where((device & 1) == 0, block, 2 * REACH - block)
    pairs = jnp.where(is_leaf, LEAF_PAIRS, UPPER_PAIRS)
    pair = (row >> 1) - jnp.where(is_leaf, UPPER_PAIRS, 0)
    swapped = (row + slot) & 1
    place_ref[...] = jnp.where(column >= 0, block * pairs + pair + 4096 * swapped, 7 * pairs)


def transpose_tiles(duo, tiles_ref, out_ref, held, stage, sem, beside):
    per_slot = K // DEPTH

    def copy(i):
        slot, part = i // per_slot, pl.ds(i % per_slot * DEPTH, DEPTH)
        return pltpu.make_async_copy(tiles_ref.at[:, 2 * duo + slot, part], held.at[:, slot, part], sem.at[i])

    for i in range(CHUNKS):
        copy(i).start()
    beside()

    def step(i, carry):
        copy(i).wait()
        slot, base = i // per_slot, i % per_slot * DEPTH
        for k in range(DEPTH):
            slab = held[:, slot, base + k].reshape(LANES, NODES).astype(F32)
            stage[pl.ds(k, NODES, stride=STRIDE), :] = slab.T
        rows = pl.ds(pl.multiple_of(i * DEPTH, DEPTH), DEPTH)
        for g in range(NODES):
            out_ref[g, rows, :] = stage[pl.ds(g * STRIDE, DEPTH), :].astype(BF16)
        return carry

    lax.fori_loop(0, CHUNKS, step, 0)


TRANSPOSE_SCRATCH = [
    pltpu.VMEM((2, 2, K, K, NODES), BF16),
    pltpu.VMEM((NODES * STRIDE + 8, LANES), F32),
    pltpu.SemaphoreType.DMA((CHUNKS,)),
]


def first_weights_kernel(tiles_ref, cols_ref, device_ref, out_ref, place_ref, cols, held, stage, sem, cols_sem):
    cols_copy = pltpu.make_async_copy(cols_ref, cols, cols_sem)
    transpose_tiles(0, tiles_ref, out_ref, held, stage, sem, cols_copy.start)
    cols_copy.wait()
    places(cols, device_ref, place_ref)


def first_weights(slabs, cols, device):
    return pl.pallas_call(
        first_weights_kernel,
        in_specs=[IN_HBM, IN_HBM, IN_SMEM],
        out_specs=(WHOLE, WHOLE),
        out_shape=(
            pltpu.VMEM((NODES, 2 * K, LANES), BF16),
            jax.ShapeDtypeStruct((SLOTS, NODES), jnp.int32),
        ),
        scratch_shapes=[pltpu.VMEM((SLOTS, NODES), jnp.int32), *TRANSPOSE_SCRATCH, pltpu.SemaphoreType.DMA],
        compiler_params=params(12),
    )(in_hbm(slabs), in_hbm(cols.T), device)


def swap_halves(pair):
    return pltpu.roll(pair, K, 1)


def fill_block(table, block, number, pairs, first=0):
    for i in range(pairs):
        pair = block[first + i]
        table[0, number * pairs + i] = pair
        table[1, number * pairs + i] = swap_halves(pair)


def fill_first(own_ref, near_ref, next_ref, table_ref, sent_ref, pairs):
    for place, (number, block) in enumerate(((REACH, own_ref), (REACH - 1, near_ref), (REACH - 2, next_ref))):
        fill_block(table_ref, block, number, pairs)
        for i in range(pairs):
            sent_ref[place * pairs + i] = block[i]
    for half in range(2):
        table_ref[half, 7 * pairs] = jnp.zeros((ROWS, LANES), BF16)


def table_and_sent(pairs):
    return (
        pltpu.VMEM((2, 7 * pairs + 1, ROWS, LANES), BF16),
        pltpu.VMEM((3 * pairs, ROWS, LANES), BF16),
    )


def second_weights_kernel(tiles_ref, own_ref, near_ref, next_ref, out_ref, table_ref, sent_ref, held, stage, sem):
    def beside():
        fill_first(own_ref, near_ref, next_ref, table_ref, sent_ref, LEAF_PAIRS)

    transpose_tiles(1, tiles_ref, out_ref, held, stage, sem, beside)


def second_weights(slabs, own, near, next_near):
    return pl.pallas_call(
        second_weights_kernel,
        in_specs=[IN_HBM, WHOLE, WHOLE, WHOLE],
        out_specs=(WHOLE, WHOLE, WHOLE),
        out_shape=(pltpu.VMEM((NODES, 2 * K, LANES), BF16), *table_and_sent(LEAF_PAIRS)),
        scratch_shapes=TRANSPOSE_SCRATCH,
        compiler_params=params(12),
    )(in_hbm(slabs), *in_vmem(own, near, next_near))


def upper_table_kernel(own_ref, near_ref, next_ref, table_ref, sent_ref):
    fill_first(own_ref, near_ref, next_ref, table_ref, sent_ref, UPPER_PAIRS)


def upper_table(own, near, next_near):
    return pl.pallas_call(
        upper_table_kernel,
        in_specs=[WHOLE, WHOLE, WHOLE],
        out_specs=(WHOLE, WHOLE),
        out_shape=table_and_sent(UPPER_PAIRS),
        compiler_params=params(4),
    )(*in_vmem(own, near, next_near))


def fill_rest(table, far_ref, other_ref, pairs):
    fill_block(table, far_ref, 0, pairs)
    for step in range(REACH):
        fill_block(table, other_ref, REACH + 1 + step, pairs, step * pairs)


def couple_pair(j, first_node, place_ref, table, weights_refs):
    low = lax.broadcasted_iota(jnp.int32, (ROWS, LANES), 1) < K

    def fetch(slot, node):
        place = place_ref[slot, node]
        return table[place >> 12, place & 4095]

    products = []
    for side in range(2):
        node = first_node + 2 * j + side
        total = None
        for duo in range(DUOS):
            halves = []
            for half in range(2):
                slot = half * 4 + duo * 2
                halves.append(jnp.where(low, fetch(slot, node), fetch(slot + 1, node)))
            operand = jnp.concatenate(halves, axis=0)
            term = jnp.dot(operand, weights_refs[duo][node], preferred_element_type=F32)
            total = term if total is None else total + term
        products.append(total)
    even, odd = products
    straight = jnp.where(low, even[:ROWS], odd[ROWS:])
    crossed = jnp.where(low, odd[:ROWS], even[ROWS:])
    return straight + swap_halves(crossed)


def leaf_kernel(place_ref, far_ref, other_ref, first_ref, second_ref, given_ref, out_ref, table):
    fill_rest(table, far_ref, other_ref, LEAF_PAIRS)

    def one(j):
        out_ref[j] = couple_pair(j, 2 * UPPER_PAIRS, place_ref, table, (first_ref, second_ref))

    each(LEAF_PAIRS, LEAF_PAIRS, one)


def leaf_level(place, far, other, weights, table):
    return pl.pallas_call(
        leaf_kernel,
        in_specs=[IN_SMEM] + [WHOLE] * 5,
        out_specs=(WHOLE, WHOLE),
        out_shape=(pltpu.VMEM((LEAF_PAIRS, ROWS, LANES), F32), table_and_sent(LEAF_PAIRS)[0]),
        input_output_aliases={5: 1},
        compiler_params=params(4),
    )(place, *in_vmem(far, other, *weights, table))[0]


OUT_PARTS = 4
OUT_STEP = LEAF_PAIRS // 2 // OUT_PARTS


def upper_kernel(place_ref, far_ref, other_ref, first_ref, second_ref, basis_ref, leaf_ref, given_ref, out_hbm, table, local, out_ref, out_sem):
    fill_rest(table, far_ref, other_ref, UPPER_PAIRS)

    def one(j):
        local[j] = couple_pair(j, 0, place_ref, table, (first_ref, second_ref))

    each(UPPER_PAIRS, UPPER_PAIRS, one)
    def put(part):
        rows = pl.ds(part * 4 * OUT_STEP, 4 * OUT_STEP)
        return pltpu.make_async_copy(out_ref.at[rows], out_hbm.at[rows], out_sem.at[part])

    contract = (((1,), (1,)), ((), ()))
    for level in range(LEV - 1):
        first = pair_offset(level)
        below = pair_offset(level + 1)
        for i in range(2**level):
            parent = local[first + i].astype(BF16)
            children = lax.dot_general(parent, basis_ref[first + i], contract, preferred_element_type=F32)
            for side in range(2):
                part = children[:, side * LANES : (side + 1) * LANES]
                if level == LEV - 2:
                    pair = part + leaf_ref[2 * i + side]
                    out_ref[4 * i + 2 * side] = pair[:, :K]
                    out_ref[4 * i + 2 * side + 1] = swap_halves(pair)[:, :K]
                else:
                    local[below + 2 * i + side] += part
            if level == LEV - 2 and (i + 1) % OUT_STEP == 0:
                put(i // OUT_STEP).start()
    for part in range(OUT_PARTS):
        put(part).wait()


def upper_levels(place, far, other, weights, basis, leaf, table):
    return pl.pallas_call(
        upper_kernel,
        in_specs=[IN_SMEM] + [WHOLE] * 7,
        out_specs=(IN_HBM, WHOLE),
        out_shape=(
            jax.ShapeDtypeStruct((2 * LEAF_PAIRS, ROWS, K), F32),
            table_and_sent(UPPER_PAIRS)[0],
        ),
        input_output_aliases={7: 1},
        scratch_shapes=[
            pltpu.VMEM((UPPER_PAIRS, ROWS, LANES), F32),
            pltpu.VMEM((2 * LEAF_PAIRS, ROWS, K), F32),
            pltpu.SemaphoreType.DMA((OUT_PARTS,)),
        ],
        compiler_params=params(6),
    )(place, *in_vmem(far, other, *weights, basis, leaf, table))[0]


def shards(leaf_skel, transfer, tiles, cols):
    count = lax.axis_size("clus")
    own_index = lax.axis_index("clus")

    def moved(block, target):
        return lax.ppermute(block, "clus", [(i, target(i) % count) for i in range(count)])

    def other_core(i):
        return i ^ 1

    def outward(i):
        return i + 2 if i % 2 == 0 else i - 2

    def across(i):
        return i + 1 if i % 2 == 1 else i - 1

    slabs = jnp.transpose(tiles, (1, 2, 3, 0)).reshape(2, SLOTS // 2, K, K, NODES)
    leaf, coeffs = front(leaf_skel, jnp.transpose(transfer, (1, 2, 0)))
    near_leaf, next_leaf = moved(leaf, across), moved(leaf, outward)
    basis, upper = upward(coeffs, leaf)
    near_upper, next_upper = moved(upper, across), moved(upper, outward)
    cols, upper = lax.optimization_barrier((cols, upper))
    first, place = first_weights(slabs, cols, own_index.astype(jnp.int32).reshape(1))
    near_leaf, next_leaf, place = lax.optimization_barrier((near_leaf, next_leaf, place))
    far_leaf = moved(near_leaf, outward)
    second, leaf_table, sent_leaf = second_weights(slabs, leaf, near_leaf, next_leaf)
    other_leaf = moved(sent_leaf, other_core)
    far_upper = moved(near_upper, outward)
    table, sent_upper = upper_table(upper, near_upper, next_upper)
    other_upper = moved(sent_upper, other_core)
    weights = (first, second)
    leaf_local = leaf_level(place, far_leaf, other_leaf, weights, leaf_table)
    return upper_levels(place, far_upper, other_upper, weights, basis, leaf_local, table)


def solution(mesh):
    in_specs = (
        P("clus", "rhs", None),
        P("clus", None, None),
        P("clus", None, None, None),
        P("clus", None),
    )
    out_specs = P("clus", "rhs", None)
    return jax.shard_map(shards, mesh=mesh, in_specs=in_specs, out_specs=out_specs, check_vma=False)
```

```python
import functools

import jax
import jax.numpy as jnp
from jax import lax
from jax.experimental import pallas as pl
from jax.experimental.pallas import tpu as pltpu
from jax.sharding import PartitionSpec as P

LEV = 6
REACH = 3
SLOTS = 8
K = 64
LANES = 128
LEAF_PAIRS = 32
UPPER_PAIRS = 31
PAIRS = LEAF_PAIRS + UPPER_PAIRS
NODES = 126
ROWS = 32
MIB = 2**20
BF16 = jnp.bfloat16
F32 = jnp.float32
WHOLE = pl.BlockSpec(memory_space=pltpu.VMEM)
IN_HBM = pl.BlockSpec(memory_space=pltpu.HBM)
IN_SMEM = pl.BlockSpec(memory_space=pltpu.SMEM)


def pair_offset(level):
    return 2**level - 1


def in_hbm(array):
    return pltpu.with_memory_space_constraint(array, pltpu.HBM)


def in_vmem(*arrays):
    return tuple(pltpu.with_memory_space_constraint(array, pltpu.VMEM) for array in arrays)


def params(mib):
    return pltpu.CompilerParams(vmem_limit_bytes=mib * MIB)


def each(count, width, body):
    def several(i, carry):
        for u in range(width):
            body(i * width + u)
        return carry

    lax.fori_loop(0, count // width, several, 0)
    for i in range(count // width * width, count):
        body(i)


def front_kernel(leaf_ref, coeff_ref, out_ref, held_ref, leaf, sems):
    first = pltpu.make_async_copy(leaf_ref, leaf, sems.at[0])
    second = pltpu.make_async_copy(coeff_ref, held_ref, sems.at[1])
    first.start()
    second.start()
    first.wait()
    for j in range(LEAF_PAIRS):
        out_ref[j] = jnp.concatenate([leaf[2 * j], leaf[2 * j + 1]], axis=1)
    second.wait()


def front(leaf, coeffs):
    return pl.pallas_call(
        front_kernel,
        in_specs=[IN_HBM, IN_HBM],
        out_specs=(WHOLE, WHOLE),
        out_shape=(pltpu.VMEM((LEAF_PAIRS, ROWS, LANES), BF16), pltpu.VMEM(coeffs.shape, BF16)),
        scratch_shapes=[pltpu.VMEM(leaf.shape, BF16), pltpu.SemaphoreType.DMA((2,))],
        compiler_params=params(8),
    )(in_hbm(leaf), in_hbm(coeffs))


E_STRIDE = K + 1
E_NODES = NODES - 2


def upward_kernel(coeff_ref, leaf_ref, basis_ref, skel_ref, stage):
    node = lax.broadcasted_iota(jnp.int32, (E_NODES, LANES), 0)
    lane = lax.broadcasted_iota(jnp.int32, (E_NODES, LANES), 1)
    own = ((node // 2) % 2) == (lane // K)
    for a in range(K):
        slab = coeff_ref[a].astype(F32)
        twice = jnp.concatenate([slab, slab], axis=0).T
        stage[pl.ds(a, E_NODES, stride=E_STRIDE), :] = jnp.where(own, twice, 0.0)
    for g in range(E_NODES):
        basis_ref[g // 4, (g % 4) * K : (g % 4 + 1) * K, :] = stage[pl.ds(g * E_STRIDE, K), :].astype(BF16)
    for level in range(LEV - 2, -1, -1):
        first = pair_offset(level)
        below = pair_offset(level + 1)
        for i in range(2**level):
            if level == LEV - 2:
                left, right = leaf_ref[2 * i], leaf_ref[2 * i + 1]
            else:
                left, right = skel_ref[below + 2 * i], skel_ref[below + 2 * i + 1]
            children = jnp.concatenate([left, right], axis=1)
            parent = jnp.dot(children, basis_ref[first + i], preferred_element_type=F32)
            skel_ref[first + i] = parent.astype(BF16)


def upward(coeffs, leaf_pairs):
    return pl.pallas_call(
        upward_kernel,
        in_specs=[WHOLE, WHOLE],
        out_specs=(WHOLE, WHOLE),
        out_shape=(
            pltpu.VMEM((UPPER_PAIRS, 4 * K, LANES), BF16),
            pltpu.VMEM((UPPER_PAIRS, ROWS, LANES), BF16),
        ),
        scratch_shapes=[pltpu.VMEM((E_NODES * E_STRIDE + 8, LANES), F32)],
        compiler_params=params(14),
    )(*in_vmem(coeffs, leaf_pairs))


DEPTH = 32
CHUNKS = 2 * K // DEPTH
STRIDE = DEPTH + 1
DUOS = SLOTS // 4


def places(cols_ref, device_ref, place_ref):
    device = device_ref[0]
    column = cols_ref[...]
    slot = lax.broadcasted_iota(jnp.int32, column.shape, 0)
    is_leaf = lax.broadcasted_iota(jnp.int32, column.shape, 1) >= 2 * UPPER_PAIRS
    past = column - (device - REACH) * NODES
    block = jnp.zeros(column.shape, jnp.int32)
    for step in range(1, 2 * REACH + 1):
        block += jnp.where(past >= step * NODES, 1, 0)
    row = past - block * NODES
    block = jnp.where((device & 1) == 0, block, 2 * REACH - block)
    pairs = jnp.where(is_leaf, LEAF_PAIRS, UPPER_PAIRS)
    pair = (row >> 1) - jnp.where(is_leaf, UPPER_PAIRS, 0)
    swapped = (row + slot) & 1
    place_ref[...] = jnp.where(column >= 0, block * pairs + pair + 4096 * swapped, 7 * pairs)


def transpose_tiles(duo, tiles_ref, out_ref, held, stage, sem, beside):
    per_slot = K // DEPTH

    def copy(i):
        slot, part = i // per_slot, pl.ds(i % per_slot * DEPTH, DEPTH)
        return pltpu.make_async_copy(tiles_ref.at[:, 2 * duo + slot, part], held.at[:, slot, part], sem.at[i])

    for i in range(CHUNKS):
        copy(i).start()
    beside()

    def step(i, carry):
        copy(i).wait()
        slot, base = i // per_slot, i % per_slot * DEPTH
        for k in range(DEPTH):
            slab = held[:, slot, base + k].reshape(LANES, NODES).astype(F32)
            stage[pl.ds(k, NODES, stride=STRIDE), :] = slab.T
        rows = pl.ds(pl.multiple_of(i * DEPTH, DEPTH), DEPTH)
        for g in range(NODES):
            out_ref[g, rows, :] = stage[pl.ds(g * STRIDE, DEPTH), :].astype(BF16)
        return carry

    lax.fori_loop(0, CHUNKS, step, 0)


TRANSPOSE_SCRATCH = [
    pltpu.VMEM((2, 2, K, K, NODES), BF16),
    pltpu.VMEM((NODES * STRIDE + 8, LANES), F32),
    pltpu.SemaphoreType.DMA((CHUNKS,)),
]


def first_weights_kernel(tiles_ref, cols_ref, device_ref, out_ref, place_ref, cols, held, stage, sem, cols_sem):
    cols_copy = pltpu.make_async_copy(cols_ref, cols, cols_sem)
    transpose_tiles(0, tiles_ref, out_ref, held, stage, sem, cols_copy.start)
    cols_copy.wait()
    places(cols, device_ref, place_ref)


def first_weights(slabs, cols, device):
    return pl.pallas_call(
        first_weights_kernel,
        in_specs=[IN_HBM, IN_HBM, IN_SMEM],
        out_specs=(WHOLE, WHOLE),
        out_shape=(
            pltpu.VMEM((NODES, 2 * K, LANES), BF16),
            jax.ShapeDtypeStruct((SLOTS, NODES), jnp.int32),
        ),
        scratch_shapes=[pltpu.VMEM((SLOTS, NODES), jnp.int32), *TRANSPOSE_SCRATCH, pltpu.SemaphoreType.DMA],
        compiler_params=params(12),
    )(in_hbm(slabs), in_hbm(cols.T), device)


def swap_halves(pair):
    return pltpu.roll(pair, K, 1)


def fill_block(table, block, number, pairs, first=0):
    for i in range(pairs):
        pair = block[first + i]
        table[0, number * pairs + i] = pair
        table[1, number * pairs + i] = swap_halves(pair)


def fill_first(own_ref, near_ref, next_ref, table_ref, sent_ref, pairs):
    for place, (number, block) in enumerate(((REACH, own_ref), (REACH - 1, near_ref), (REACH - 2, next_ref))):
        fill_block(table_ref, block, number, pairs)
        for i in range(pairs):
            sent_ref[place * pairs + i] = block[i]
    for half in range(2):
        table_ref[half, 7 * pairs] = jnp.zeros((ROWS, LANES), BF16)


def table_and_sent(pairs):
    return (
        pltpu.VMEM((2, 7 * pairs + 1, ROWS, LANES), BF16),
        pltpu.VMEM((3 * pairs, ROWS, LANES), BF16),
    )


def second_weights_kernel(tiles_ref, own_ref, near_ref, next_ref, out_ref, table_ref, sent_ref, held, stage, sem):
    def beside():
        fill_first(own_ref, near_ref, next_ref, table_ref, sent_ref, LEAF_PAIRS)

    transpose_tiles(1, tiles_ref, out_ref, held, stage, sem, beside)


def second_weights(slabs, own, near, next_near):
    return pl.pallas_call(
        second_weights_kernel,
        in_specs=[IN_HBM, WHOLE, WHOLE, WHOLE],
        out_specs=(WHOLE, WHOLE, WHOLE),
        out_shape=(pltpu.VMEM((NODES, 2 * K, LANES), BF16), *table_and_sent(LEAF_PAIRS)),
        scratch_shapes=TRANSPOSE_SCRATCH,
        compiler_params=params(12),
    )(in_hbm(slabs), *in_vmem(own, near, next_near))


def upper_table_kernel(own_ref, near_ref, next_ref, table_ref, sent_ref):
    fill_first(own_ref, near_ref, next_ref, table_ref, sent_ref, UPPER_PAIRS)


def upper_table(own, near, next_near):
    return pl.pallas_call(
        upper_table_kernel,
        in_specs=[WHOLE, WHOLE, WHOLE],
        out_specs=(WHOLE, WHOLE),
        out_shape=table_and_sent(UPPER_PAIRS),
        compiler_params=params(4),
    )(*in_vmem(own, near, next_near))


def rest_kernel(leaf_ref, upper_ref, given_leaf, given_upper, leaf_table, upper_table):
    for table, other_ref, pairs in ((leaf_table, leaf_ref, LEAF_PAIRS), (upper_table, upper_ref, UPPER_PAIRS)):
        for step in range(REACH):
            fill_block(table, other_ref, REACH + 1 + step, pairs, step * pairs)


def rest_of_tables(other_leaf, other_upper, leaf_table, table):
    return pl.pallas_call(
        rest_kernel,
        in_specs=[WHOLE] * 4,
        out_specs=(WHOLE, WHOLE),
        out_shape=(table_and_sent(LEAF_PAIRS)[0], table_and_sent(UPPER_PAIRS)[0]),
        input_output_aliases={2: 0, 3: 1},
        compiler_params=params(2),
    )(*in_vmem(other_leaf, other_upper, leaf_table, table))


def couple_pair(j, first_node, place_ref, table, weights_refs):
    low = lax.broadcasted_iota(jnp.int32, (ROWS, LANES), 1) < K

    def fetch(slot, node):
        place = place_ref[slot, node]
        return table[place >> 12, place & 4095]

    products = []
    for side in range(2):
        node = first_node + 2 * j + side
        total = None
        for duo in range(DUOS):
            halves = []
            for half in range(2):
                slot = half * 4 + duo * 2
                halves.append(jnp.where(low, fetch(slot, node), fetch(slot + 1, node)))
            operand = jnp.concatenate(halves, axis=0)
            term = jnp.dot(operand, weights_refs[duo][node], preferred_element_type=F32)
            total = term if total is None else total + term
        products.append(total)
    even, odd = products
    straight = jnp.where(low, even[:ROWS], odd[ROWS:])
    crossed = jnp.where(low, odd[:ROWS], even[ROWS:])
    return straight + swap_halves(crossed)


def leaf_kernel(place_ref, far_ref, first_ref, second_ref, given_ref, out_ref, table):
    fill_block(table, far_ref, 0, LEAF_PAIRS)

    def one(j):
        out_ref[j] = couple_pair(j, 2 * UPPER_PAIRS, place_ref, table, (first_ref, second_ref))

    each(LEAF_PAIRS, LEAF_PAIRS, one)


def leaf_level(place, far, weights, table):
    return pl.pallas_call(
        leaf_kernel,
        in_specs=[IN_SMEM] + [WHOLE] * 4,
        out_specs=(WHOLE, WHOLE),
        out_shape=(pltpu.VMEM((LEAF_PAIRS, ROWS, LANES), F32), table_and_sent(LEAF_PAIRS)[0]),
        input_output_aliases={4: 1},
        compiler_params=params(4),
    )(place, *in_vmem(far, *weights, table))[0]


OUT_PARTS = 4
OUT_STEP = LEAF_PAIRS // 2 // OUT_PARTS


def upper_kernel(place_ref, far_ref, first_ref, second_ref, basis_ref, leaf_ref, given_ref, out_hbm, table, local, out_ref, out_sem):
    fill_block(table, far_ref, 0, UPPER_PAIRS)

    def one(j):
        local[j] = couple_pair(j, 0, place_ref, table, (first_ref, second_ref))

    each(UPPER_PAIRS, UPPER_PAIRS, one)
    def put(part):
        rows = pl.ds(part * 4 * OUT_STEP, 4 * OUT_STEP)
        return pltpu.make_async_copy(out_ref.at[rows], out_hbm.at[rows], out_sem.at[part])

    contract = (((1,), (1,)), ((), ()))
    for level in range(LEV - 1):
        first = pair_offset(level)
        below = pair_offset(level + 1)
        for i in range(2**level):
            parent = local[first + i].astype(BF16)
            children = lax.dot_general(parent, basis_ref[first + i], contract, preferred_element_type=F32)
            for side in range(2):
                part = children[:, side * LANES : (side + 1) * LANES]
                if level == LEV - 2:
                    pair = part + leaf_ref[2 * i + side]
                    out_ref[4 * i + 2 * side] = pair[:, :K]
                    out_ref[4 * i + 2 * side + 1] = swap_halves(pair)[:, :K]
                else:
                    local[below + 2 * i + side] += part
            if level == LEV - 2 and (i + 1) % OUT_STEP == 0:
                put(i // OUT_STEP).start()
    for part in range(OUT_PARTS):
        put(part).wait()


def upper_levels(place, far, weights, basis, leaf, table):
    return pl.pallas_call(
        upper_kernel,
        in_specs=[IN_SMEM] + [WHOLE] * 6,
        out_specs=(IN_HBM, WHOLE),
        out_shape=(
            jax.ShapeDtypeStruct((2 * LEAF_PAIRS, ROWS, K), F32),
            table_and_sent(UPPER_PAIRS)[0],
        ),
        input_output_aliases={6: 1},
        scratch_shapes=[
            pltpu.VMEM((UPPER_PAIRS, ROWS, LANES), F32),
            pltpu.VMEM((2 * LEAF_PAIRS, ROWS, K), F32),
            pltpu.SemaphoreType.DMA((OUT_PARTS,)),
        ],
        compiler_params=params(6),
    )(place, *in_vmem(far, *weights, basis, leaf, table))[0]


def shards(leaf_skel, transfer, tiles, cols):
    count = lax.axis_size("clus")
    own_index = lax.axis_index("clus")

    def moved(block, target):
        return lax.ppermute(block, "clus", [(i, target(i) % count) for i in range(count)])

    def other_core(i):
        return i ^ 1

    def outward(i):
        return i + 2 if i % 2 == 0 else i - 2

    def across(i):
        return i + 1 if i % 2 == 1 else i - 1

    slabs = jnp.transpose(tiles, (1, 2, 3, 0)).reshape(2, SLOTS // 2, K, K, NODES)
    leaf, coeffs = front(leaf_skel, jnp.transpose(transfer, (1, 2, 0)))
    near_leaf, next_leaf = moved(leaf, across), moved(leaf, outward)
    basis, upper = upward(coeffs, leaf)
    near_upper, next_upper = moved(upper, across), moved(upper, outward)
    cols, upper = lax.optimization_barrier((cols, upper))
    first, place = first_weights(slabs, cols, own_index.astype(jnp.int32).reshape(1))
    near_leaf, next_leaf, place = lax.optimization_barrier((near_leaf, next_leaf, place))
    far_leaf = moved(near_leaf, outward)
    second, leaf_table, sent_leaf = second_weights(slabs, leaf, near_leaf, next_leaf)
    other_leaf = moved(sent_leaf, other_core)
    far_upper = moved(near_upper, outward)
    table, sent_upper = upper_table(upper, near_upper, next_upper)
    other_upper = moved(sent_upper, other_core)
    leaf_table, table = rest_of_tables(other_leaf, other_upper, leaf_table, table)
    weights = (first, second)
    leaf_local = leaf_level(place, far_leaf, weights, leaf_table)
    return upper_levels(place, far_upper, weights, basis, leaf_local, table)


def solution(mesh):
    in_specs = (
        P("clus", "rhs", None),
        P("clus", None, None),
        P("clus", None, None, None),
        P("clus", None),
    )
    out_specs = P("clus", "rhs", None)
    return jax.shard_map(shards, mesh=mesh, in_specs=in_specs, out_specs=out_specs, check_vma=False)
```

```python
import functools

import jax
import jax.numpy as jnp
from jax import lax
from jax.experimental import pallas as pl
from jax.experimental.pallas import tpu as pltpu
from jax.sharding import PartitionSpec as P

LEV = 6
REACH = 3
SLOTS = 8
K = 64
LANES = 128
LEAF_PAIRS = 32
UPPER_PAIRS = 31
PAIRS = LEAF_PAIRS + UPPER_PAIRS
NODES = 126
ROWS = 32
MIB = 2**20
BF16 = jnp.bfloat16
F32 = jnp.float32
WHOLE = pl.BlockSpec(memory_space=pltpu.VMEM)
IN_HBM = pl.BlockSpec(memory_space=pltpu.HBM)
IN_SMEM = pl.BlockSpec(memory_space=pltpu.SMEM)


def pair_offset(level):
    return 2**level - 1


def in_hbm(array):
    return pltpu.with_memory_space_constraint(array, pltpu.HBM)


def in_vmem(*arrays):
    return tuple(pltpu.with_memory_space_constraint(array, pltpu.VMEM) for array in arrays)


def params(mib):
    return pltpu.CompilerParams(vmem_limit_bytes=mib * MIB)


def each(count, width, body):
    def several(i, carry):
        for u in range(width):
            body(i * width + u)
        return carry

    lax.fori_loop(0, count // width, several, 0)
    for i in range(count // width * width, count):
        body(i)


def front_kernel(leaf_ref, coeff_ref, out_ref, held_ref, leaf, sems):
    first = pltpu.make_async_copy(leaf_ref, leaf, sems.at[0])
    second = pltpu.make_async_copy(coeff_ref, held_ref, sems.at[1])
    first.start()
    second.start()
    first.wait()
    for j in range(LEAF_PAIRS):
        out_ref[j] = jnp.concatenate([leaf[2 * j], leaf[2 * j + 1]], axis=1)
    second.wait()


def front(leaf, coeffs):
    return pl.pallas_call(
        front_kernel,
        in_specs=[IN_HBM, IN_HBM],
        out_specs=(WHOLE, WHOLE),
        out_shape=(pltpu.VMEM((LEAF_PAIRS, ROWS, LANES), BF16), pltpu.VMEM(coeffs.shape, BF16)),
        scratch_shapes=[pltpu.VMEM(leaf.shape, BF16), pltpu.SemaphoreType.DMA((2,))],
        compiler_params=params(8),
    )(in_hbm(leaf), in_hbm(coeffs))


E_STRIDE = K + 1
E_NODES = NODES - 2


def upward_kernel(coeff_ref, leaf_ref, basis_ref, skel_ref, stage):
    node = lax.broadcasted_iota(jnp.int32, (E_NODES, LANES), 0)
    lane = lax.broadcasted_iota(jnp.int32, (E_NODES, LANES), 1)
    own = ((node // 2) % 2) == (lane // K)
    for a in range(K):
        slab = coeff_ref[a].astype(F32)
        twice = jnp.concatenate([slab, slab], axis=0).T
        stage[pl.ds(a, E_NODES, stride=E_STRIDE), :] = jnp.where(own, twice, 0.0)
    for g in range(E_NODES):
        basis_ref[g // 4, (g % 4) * K : (g % 4 + 1) * K, :] = stage[pl.ds(g * E_STRIDE, K), :].astype(BF16)
    for level in range(LEV - 2, -1, -1):
        first = pair_offset(level)
        below = pair_offset(level + 1)
        for i in range(2**level):
            if level == LEV - 2:
                left, right = leaf_ref[2 * i], leaf_ref[2 * i + 1]
            else:
                left, right = skel_ref[below + 2 * i], skel_ref[below + 2 * i + 1]
            children = jnp.concatenate([left, right], axis=1)
            parent = jnp.dot(children, basis_ref[first + i], preferred_element_type=F32)
            skel_ref[first + i] = parent.astype(BF16)


def upward(coeffs, leaf_pairs):
    return pl.pallas_call(
        upward_kernel,
        in_specs=[WHOLE, WHOLE],
        out_specs=(WHOLE, WHOLE),
        out_shape=(
            pltpu.VMEM((UPPER_PAIRS, 4 * K, LANES), BF16),
            pltpu.VMEM((UPPER_PAIRS, ROWS, LANES), BF16),
        ),
        scratch_shapes=[pltpu.VMEM((E_NODES * E_STRIDE + 8, LANES), F32)],
        compiler_params=params(14),
    )(*in_vmem(coeffs, leaf_pairs))


DEPTH = 32
CHUNKS = 2 * K // DEPTH
STRIDE = DEPTH + 1
DUOS = SLOTS // 4


def places(cols_ref, device_ref, place_ref):
    device = device_ref[0]
    column = cols_ref[...]
    slot = lax.broadcasted_iota(jnp.int32, column.shape, 0)
    is_leaf = lax.broadcasted_iota(jnp.int32, column.shape, 1) >= 2 * UPPER_PAIRS
    past = column - (device - REACH) * NODES
    block = jnp.zeros(column.shape, jnp.int32)
    for step in range(1, 2 * REACH + 1):
        block += jnp.where(past >= step * NODES, 1, 0)
    row = past - block * NODES
    block = jnp.where((device & 1) == 0, block, 2 * REACH - block)
    pairs = jnp.where(is_leaf, LEAF_PAIRS, UPPER_PAIRS)
    pair = (row >> 1) - jnp.where(is_leaf, UPPER_PAIRS, 0)
    swapped = (row + slot) & 1
    place_ref[...] = jnp.where(column >= 0, block * pairs + pair + 4096 * swapped, 7 * pairs)


def transpose_tiles(duo, tiles_ref, out_ref, held, stage, sem, beside):
    per_slot = K // DEPTH

    def copy(i):
        slot, part = i // per_slot, pl.ds(i % per_slot * DEPTH, DEPTH)
        return pltpu.make_async_copy(tiles_ref.at[:, 2 * duo + slot, part], held.at[:, slot, part], sem.at[i])

    for i in range(CHUNKS):
        copy(i).start()
    beside()

    def step(i, carry):
        copy(i).wait()
        slot, base = i // per_slot, i % per_slot * DEPTH
        for k in range(DEPTH):
            slab = held[:, slot, base + k].reshape(LANES, NODES).astype(F32)
            stage[pl.ds(k, NODES, stride=STRIDE), :] = slab.T
        rows = pl.ds(pl.multiple_of(i * DEPTH, DEPTH), DEPTH)
        for g in range(NODES):
            out_ref[g, rows, :] = stage[pl.ds(g * STRIDE, DEPTH), :].astype(BF16)
        return carry

    lax.fori_loop(0, CHUNKS, step, 0)


TRANSPOSE_SCRATCH = [
    pltpu.VMEM((2, 2, K, K, NODES), BF16),
    pltpu.VMEM((NODES * STRIDE + 8, LANES), F32),
    pltpu.SemaphoreType.DMA((CHUNKS,)),
]


def first_weights_kernel(tiles_ref, cols_ref, device_ref, out_ref, place_ref, cols, held, stage, sem, cols_sem):
    cols_copy = pltpu.make_async_copy(cols_ref, cols, cols_sem)
    transpose_tiles(0, tiles_ref, out_ref, held, stage, sem, cols_copy.start)
    cols_copy.wait()
    places(cols, device_ref, place_ref)


def first_weights(slabs, cols, device):
    return pl.pallas_call(
        first_weights_kernel,
        in_specs=[IN_HBM, IN_HBM, IN_SMEM],
        out_specs=(WHOLE, WHOLE),
        out_shape=(
            pltpu.VMEM((NODES, 2 * K, LANES), BF16),
            jax.ShapeDtypeStruct((SLOTS, NODES), jnp.int32),
        ),
        scratch_shapes=[pltpu.VMEM((SLOTS, NODES), jnp.int32), *TRANSPOSE_SCRATCH, pltpu.SemaphoreType.DMA],
        compiler_params=params(12),
    )(in_hbm(slabs), in_hbm(cols.T), device)


def swap_halves(pair):
    return pltpu.roll(pair, K, 1)


def fill_block(table, block, number, pairs, first=0):
    for i in range(pairs):
        pair = block[first + i]
        table[0, number * pairs + i] = pair
        table[1, number * pairs + i] = swap_halves(pair)


def fill_first(own_ref, near_ref, next_ref, table_ref, sent_ref, pairs):
    for place, (number, block) in enumerate(((REACH, own_ref), (REACH - 1, near_ref), (REACH - 2, next_ref))):
        fill_block(table_ref, block, number, pairs)
        for i in range(pairs):
            sent_ref[place * pairs + i] = block[i]
    for half in range(2):
        table_ref[half, 7 * pairs] = jnp.zeros((ROWS, LANES), BF16)


def table_and_sent(pairs):
    return (
        pltpu.VMEM((2, 7 * pairs + 1, ROWS, LANES), BF16),
        pltpu.VMEM((3 * pairs, ROWS, LANES), BF16),
    )


def second_weights_kernel(
    tiles_ref, own_ref, near_ref, next_ref, out_ref, table_ref, sent_ref, held, stage, sem, next_sem
):
    last = sent_ref.at[pl.ds(2 * LEAF_PAIRS, LEAF_PAIRS)]
    next_copy = pltpu.make_async_copy(next_ref, last, next_sem)
    next_copy.start()

    def beside():
        for place, (number, block) in enumerate(((REACH, own_ref), (REACH - 1, near_ref))):
            fill_block(table_ref, block, number, LEAF_PAIRS)
            for i in range(LEAF_PAIRS):
                sent_ref[place * LEAF_PAIRS + i] = block[i]
        for half in range(2):
            table_ref[half, 7 * LEAF_PAIRS] = jnp.zeros((ROWS, LANES), BF16)
        next_copy.wait()
        fill_block(table_ref, sent_ref, REACH - 2, LEAF_PAIRS, 2 * LEAF_PAIRS)

    transpose_tiles(1, tiles_ref, out_ref, held, stage, sem, beside)


def second_weights(slabs, own, near, next_near):
    return pl.pallas_call(
        second_weights_kernel,
        in_specs=[IN_HBM, WHOLE, WHOLE, IN_HBM],
        out_specs=(WHOLE, WHOLE, WHOLE),
        out_shape=(pltpu.VMEM((NODES, 2 * K, LANES), BF16), *table_and_sent(LEAF_PAIRS)),
        scratch_shapes=[*TRANSPOSE_SCRATCH, pltpu.SemaphoreType.DMA],
        compiler_params=params(12),
    )(in_hbm(slabs), *in_vmem(own, near), in_hbm(next_near))


def upper_table_kernel(own_ref, near_ref, next_ref, table_ref, sent_ref):
    fill_first(own_ref, near_ref, next_ref, table_ref, sent_ref, UPPER_PAIRS)


def upper_table(own, near, next_near):
    return pl.pallas_call(
        upper_table_kernel,
        in_specs=[WHOLE, WHOLE, WHOLE],
        out_specs=(WHOLE, WHOLE),
        out_shape=table_and_sent(UPPER_PAIRS),
        compiler_params=params(4),
    )(*in_vmem(own, near, next_near))


def rest_kernel(leaf_ref, upper_ref, given_leaf, given_upper, leaf_table, upper_table):
    for table, other_ref, pairs in ((leaf_table, leaf_ref, LEAF_PAIRS), (upper_table, upper_ref, UPPER_PAIRS)):
        for step in range(REACH):
            fill_block(table, other_ref, REACH + 1 + step, pairs, step * pairs)


def rest_of_tables(other_leaf, other_upper, leaf_table, table):
    return pl.pallas_call(
        rest_kernel,
        in_specs=[WHOLE] * 4,
        out_specs=(WHOLE, WHOLE),
        out_shape=(table_and_sent(LEAF_PAIRS)[0], table_and_sent(UPPER_PAIRS)[0]),
        input_output_aliases={2: 0, 3: 1},
        compiler_params=params(2),
    )(*in_vmem(other_leaf, other_upper, leaf_table, table))


def couple_pair(j, first_node, place_ref, table, weights_refs):
    low = lax.broadcasted_iota(jnp.int32, (ROWS, LANES), 1) < K

    def fetch(slot, node):
        place = place_ref[slot, node]
        return table[place >> 12, place & 4095]

    products = []
    for side in range(2):
        node = first_node + 2 * j + side
        total = None
        for duo in range(DUOS):
            halves = []
            for half in range(2):
                slot = half * 4 + duo * 2
                halves.append(jnp.where(low, fetch(slot, node), fetch(slot + 1, node)))
            operand = jnp.concatenate(halves, axis=0)
            term = jnp.dot(operand, weights_refs[duo][node], preferred_element_type=F32)
            total = term if total is None else total + term
        products.append(total)
    even, odd = products
    straight = jnp.where(low, even[:ROWS], odd[ROWS:])
    crossed = jnp.where(low, odd[:ROWS], even[ROWS:])
    return straight + swap_halves(crossed)


def leaf_kernel(place_ref, far_ref, first_ref, second_ref, given_ref, out_ref, table):
    fill_block(table, far_ref, 0, LEAF_PAIRS)

    def one(j):
        out_ref[j] = couple_pair(j, 2 * UPPER_PAIRS, place_ref, table, (first_ref, second_ref))

    each(LEAF_PAIRS, LEAF_PAIRS, one)


def leaf_level(place, far, weights, table):
    return pl.pallas_call(
        leaf_kernel,
        in_specs=[IN_SMEM] + [WHOLE] * 4,
        out_specs=(WHOLE, WHOLE),
        out_shape=(pltpu.VMEM((LEAF_PAIRS, ROWS, LANES), F32), table_and_sent(LEAF_PAIRS)[0]),
        input_output_aliases={4: 1},
        compiler_params=params(4),
    )(place, *in_vmem(far, *weights, table))[0]


OUT_PARTS = 4
OUT_STEP = LEAF_PAIRS // 2 // OUT_PARTS


def upper_kernel(place_ref, far_ref, first_ref, second_ref, basis_ref, leaf_ref, given_ref, out_hbm, table, local, out_ref, out_sem):
    fill_block(table, far_ref, 0, UPPER_PAIRS)

    def one(j):
        local[j] = couple_pair(j, 0, place_ref, table, (first_ref, second_ref))

    each(UPPER_PAIRS, UPPER_PAIRS, one)
    def put(part):
        rows = pl.ds(part * 4 * OUT_STEP, 4 * OUT_STEP)
        return pltpu.make_async_copy(out_ref.at[rows], out_hbm.at[rows], out_sem.at[part])

    contract = (((1,), (1,)), ((), ()))
    for level in range(LEV - 1):
        first = pair_offset(level)
        below = pair_offset(level + 1)
        for i in range(2**level):
            parent = local[first + i].astype(BF16)
            children = lax.dot_general(parent, basis_ref[first + i], contract, preferred_element_type=F32)
            for side in range(2):
                part = children[:, side * LANES : (side + 1) * LANES]
                if level == LEV - 2:
                    pair = part + leaf_ref[2 * i + side]
                    out_ref[4 * i + 2 * side] = pair[:, :K]
                    out_ref[4 * i + 2 * side + 1] = swap_halves(pair)[:, :K]
                else:
                    local[below + 2 * i + side] += part
            if level == LEV - 2 and (i + 1) % OUT_STEP == 0:
                put(i // OUT_STEP).start()
    for part in range(OUT_PARTS):
        put(part).wait()


def upper_levels(place, far, weights, basis, leaf, table):
    return pl.pallas_call(
        upper_kernel,
        in_specs=[IN_SMEM] + [WHOLE] * 6,
        out_specs=(IN_HBM, WHOLE),
        out_shape=(
            jax.ShapeDtypeStruct((2 * LEAF_PAIRS, ROWS, K), F32),
            table_and_sent(UPPER_PAIRS)[0],
        ),
        input_output_aliases={6: 1},
        scratch_shapes=[
            pltpu.VMEM((UPPER_PAIRS, ROWS, LANES), F32),
            pltpu.VMEM((2 * LEAF_PAIRS, ROWS, K), F32),
            pltpu.SemaphoreType.DMA((OUT_PARTS,)),
        ],
        compiler_params=params(6),
    )(place, *in_vmem(far, *weights, basis, leaf, table))[0]


def shards(leaf_skel, transfer, tiles, cols):
    count = lax.axis_size("clus")
    own_index = lax.axis_index("clus")

    def moved(block, target):
        return lax.ppermute(block, "clus", [(i, target(i) % count) for i in range(count)])

    def other_core(i):
        return i ^ 1

    def outward(i):
        return i + 2 if i % 2 == 0 else i - 2

    def across(i):
        return i + 1 if i % 2 == 1 else i - 1

    slabs = jnp.transpose(tiles, (1, 2, 3, 0)).reshape(2, SLOTS // 2, K, K, NODES)
    leaf, coeffs = front(leaf_skel, jnp.transpose(transfer, (1, 2, 0)))
    near_leaf, next_leaf = moved(leaf, across), moved(leaf, outward)
    basis, upper = upward(coeffs, leaf)
    near_upper, next_upper = moved(upper, across), moved(upper, outward)
    cols, upper = lax.optimization_barrier((cols, upper))
    first, place = first_weights(slabs, cols, own_index.astype(jnp.int32).reshape(1))
    near_leaf, next_leaf, place = lax.optimization_barrier((near_leaf, next_leaf, place))
    far_leaf = moved(near_leaf, outward)
    second, leaf_table, sent_leaf = second_weights(slabs, leaf, near_leaf, next_leaf)
    other_leaf = moved(sent_leaf, other_core)
    far_upper = moved(near_upper, outward)
    table, sent_upper = upper_table(upper, near_upper, next_upper)
    other_upper = moved(sent_upper, other_core)
    leaf_table, table = rest_of_tables(other_leaf, other_upper, leaf_table, table)
    weights = (first, second)
    leaf_local = leaf_level(place, far_leaf, weights, leaf_table)
    return upper_levels(place, far_upper, weights, basis, leaf_local, table)


def solution(mesh):
    in_specs = (
        P("clus", "rhs", None),
        P("clus", None, None),
        P("clus", None, None, None),
        P("clus", None),
    )
    out_specs = P("clus", "rhs", None)
    return jax.shard_map(shards, mesh=mesh, in_specs=in_specs, out_specs=out_specs, check_vma=False)
```

```python
import functools

import jax
import jax.numpy as jnp
from jax import lax
from jax.experimental import pallas as pl
from jax.experimental.pallas import tpu as pltpu
from jax.sharding import PartitionSpec as P

LEV = 6
REACH = 3
SLOTS = 8
K = 64
LANES = 128
LEAF_PAIRS = 32
UPPER_PAIRS = 31
PAIRS = LEAF_PAIRS + UPPER_PAIRS
NODES = 126
ROWS = 32
MIB = 2**20
BF16 = jnp.bfloat16
F32 = jnp.float32
WHOLE = pl.BlockSpec(memory_space=pltpu.VMEM)
IN_HBM = pl.BlockSpec(memory_space=pltpu.HBM)
IN_SMEM = pl.BlockSpec(memory_space=pltpu.SMEM)


def pair_offset(level):
    return 2**level - 1


def in_hbm(array):
    return pltpu.with_memory_space_constraint(array, pltpu.HBM)


def in_vmem(*arrays):
    return tuple(pltpu.with_memory_space_constraint(array, pltpu.VMEM) for array in arrays)


def params(mib):
    return pltpu.CompilerParams(vmem_limit_bytes=mib * MIB)


def each(count, width, body):
    def several(i, carry):
        for u in range(width):
            body(i * width + u)
        return carry

    lax.fori_loop(0, count // width, several, 0)
    for i in range(count // width * width, count):
        body(i)


def front_kernel(leaf_ref, coeff_ref, out_ref, held_ref, leaf, sems):
    first = pltpu.make_async_copy(leaf_ref, leaf, sems.at[0])
    second = pltpu.make_async_copy(coeff_ref, held_ref, sems.at[1])
    first.start()
    second.start()
    first.wait()
    for j in range(LEAF_PAIRS):
        out_ref[j] = jnp.concatenate([leaf[2 * j], leaf[2 * j + 1]], axis=1)
    second.wait()


def front(leaf, coeffs):
    return pl.pallas_call(
        front_kernel,
        in_specs=[IN_HBM, IN_HBM],
        out_specs=(WHOLE, WHOLE),
        out_shape=(pltpu.VMEM((LEAF_PAIRS, ROWS, LANES), BF16), pltpu.VMEM(coeffs.shape, BF16)),
        scratch_shapes=[pltpu.VMEM(leaf.shape, BF16), pltpu.SemaphoreType.DMA((2,))],
        compiler_params=params(8),
    )(in_hbm(leaf), in_hbm(coeffs))


E_STRIDE = K + 1
E_NODES = NODES - 2


def upward_kernel(coeff_ref, leaf_ref, basis_ref, skel_ref, stage):
    node = lax.broadcasted_iota(jnp.int32, (E_NODES, LANES), 0)
    lane = lax.broadcasted_iota(jnp.int32, (E_NODES, LANES), 1)
    own = ((node // 2) % 2) == (lane // K)
    for a in range(K):
        slab = coeff_ref[a].astype(F32)
        twice = jnp.concatenate([slab, slab], axis=0).T
        stage[pl.ds(a, E_NODES, stride=E_STRIDE), :] = jnp.where(own, twice, 0.0)
    for g in range(E_NODES):
        basis_ref[g // 4, (g % 4) * K : (g % 4 + 1) * K, :] = stage[pl.ds(g * E_STRIDE, K), :].astype(BF16)
    for level in range(LEV - 2, -1, -1):
        first = pair_offset(level)
        below = pair_offset(level + 1)
        for i in range(2**level):
            if level == LEV - 2:
                left, right = leaf_ref[2 * i], leaf_ref[2 * i + 1]
            else:
                left, right = skel_ref[below + 2 * i], skel_ref[below + 2 * i + 1]
            children = jnp.concatenate([left, right], axis=1)
            parent = jnp.dot(children, basis_ref[first + i], preferred_element_type=F32)
            skel_ref[first + i] = parent.astype(BF16)


def upward(coeffs, leaf_pairs):
    return pl.pallas_call(
        upward_kernel,
        in_specs=[WHOLE, WHOLE],
        out_specs=(WHOLE, WHOLE),
        out_shape=(
            pltpu.VMEM((UPPER_PAIRS, 4 * K, LANES), BF16),
            pltpu.VMEM((UPPER_PAIRS, ROWS, LANES), BF16),
        ),
        scratch_shapes=[pltpu.VMEM((LANES * E_STRIDE + 8, LANES), F32)],
        compiler_params=params(14),
    )(*in_vmem(coeffs, leaf_pairs))


DEPTH = 32
CHUNKS = 2 * K // DEPTH
STRIDE = DEPTH + 1
DUOS = SLOTS // 4


def places(cols_ref, device_ref, place_ref):
    device = device_ref[0]
    column = cols_ref[...]
    slot = lax.broadcasted_iota(jnp.int32, column.shape, 0)
    is_leaf = lax.broadcasted_iota(jnp.int32, column.shape, 1) >= 2 * UPPER_PAIRS
    past = column - (device - REACH) * NODES
    block = jnp.zeros(column.shape, jnp.int32)
    for step in range(1, 2 * REACH + 1):
        block += jnp.where(past >= step * NODES, 1, 0)
    row = past - block * NODES
    block = jnp.where((device & 1) == 0, block, 2 * REACH - block)
    pairs = jnp.where(is_leaf, LEAF_PAIRS, UPPER_PAIRS)
    pair = (row >> 1) - jnp.where(is_leaf, UPPER_PAIRS, 0)
    swapped = (row + slot) & 1
    place_ref[...] = jnp.where(column >= 0, block * pairs + pair + 4096 * swapped, 7 * pairs)


def transpose_tiles(duo, tiles_ref, out_ref, held, stage, sem, beside):
    per_slot = K // DEPTH

    def copy(i):
        slot, part = i // per_slot, pl.ds(i % per_slot * DEPTH, DEPTH)
        return pltpu.make_async_copy(tiles_ref.at[:, 2 * duo + slot, part], held.at[:, slot, part], sem.at[i])

    for i in range(CHUNKS):
        copy(i).start()
    beside()

    def step(i, carry):
        copy(i).wait()
        slot, base = i // per_slot, i % per_slot * DEPTH
        for k in range(DEPTH):
            slab = held[:, slot, base + k].reshape(LANES, NODES).astype(F32)
            stage[pl.ds(k, NODES, stride=STRIDE), :] = slab.T
        rows = pl.ds(pl.multiple_of(i * DEPTH, DEPTH), DEPTH)
        for g in range(NODES):
            out_ref[g, rows, :] = stage[pl.ds(g * STRIDE, DEPTH), :].astype(BF16)
        return carry

    lax.fori_loop(0, CHUNKS, step, 0)


TRANSPOSE_SCRATCH = [
    pltpu.VMEM((2, 2, K, K, NODES), BF16),
    pltpu.VMEM((LANES * STRIDE + 8, LANES), F32),
    pltpu.SemaphoreType.DMA((CHUNKS,)),
]


def first_weights_kernel(tiles_ref, cols_ref, device_ref, out_ref, place_ref, cols, held, stage, sem, cols_sem):
    cols_copy = pltpu.make_async_copy(cols_ref, cols, cols_sem)
    transpose_tiles(0, tiles_ref, out_ref, held, stage, sem, cols_copy.start)
    cols_copy.wait()
    places(cols, device_ref, place_ref)


def first_weights(slabs, cols, device):
    return pl.pallas_call(
        first_weights_kernel,
        in_specs=[IN_HBM, IN_HBM, IN_SMEM],
        out_specs=(WHOLE, WHOLE),
        out_shape=(
            pltpu.VMEM((NODES, 2 * K, LANES), BF16),
            jax.ShapeDtypeStruct((SLOTS, NODES), jnp.int32),
        ),
        scratch_shapes=[pltpu.VMEM((SLOTS, NODES), jnp.int32), *TRANSPOSE_SCRATCH, pltpu.SemaphoreType.DMA],
        compiler_params=params(12),
    )(in_hbm(slabs), in_hbm(cols.T), device)


def swap_halves(pair):
    return pltpu.roll(pair, K, 1)


def fill_block(table, block, number, pairs, first=0):
    for i in range(pairs):
        pair = block[first + i]
        table[0, number * pairs + i] = pair
        table[1, number * pairs + i] = swap_halves(pair)


def fill_first(own_ref, near_ref, next_ref, table_ref, sent_ref, pairs):
    for place, (number, block) in enumerate(((REACH, own_ref), (REACH - 1, near_ref), (REACH - 2, next_ref))):
        fill_block(table_ref, block, number, pairs)
        for i in range(pairs):
            sent_ref[place * pairs + i] = block[i]
    for half in range(2):
        table_ref[half, 7 * pairs] = jnp.zeros((ROWS, LANES), BF16)


def table_and_sent(pairs):
    return (
        pltpu.VMEM((2, 7 * pairs + 1, ROWS, LANES), BF16),
        pltpu.VMEM((3 * pairs, ROWS, LANES), BF16),
    )


def second_weights_kernel(
    tiles_ref, own_ref, near_ref, next_ref, out_ref, table_ref, sent_ref, held, stage, sem, next_sem
):
    last = sent_ref.at[pl.ds(2 * LEAF_PAIRS, LEAF_PAIRS)]
    next_copy = pltpu.make_async_copy(next_ref, last, next_sem)
    next_copy.start()

    def beside():
        for place, (number, block) in enumerate(((REACH, own_ref), (REACH - 1, near_ref))):
            fill_block(table_ref, block, number, LEAF_PAIRS)
            for i in range(LEAF_PAIRS):
                sent_ref[place * LEAF_PAIRS + i] = block[i]
        for half in range(2):
            table_ref[half, 7 * LEAF_PAIRS] = jnp.zeros((ROWS, LANES), BF16)
        next_copy.wait()
        fill_block(table_ref, sent_ref, REACH - 2, LEAF_PAIRS, 2 * LEAF_PAIRS)

    transpose_tiles(1, tiles_ref, out_ref, held, stage, sem, beside)


def second_weights(slabs, own, near, next_near):
    return pl.pallas_call(
        second_weights_kernel,
        in_specs=[IN_HBM, WHOLE, WHOLE, IN_HBM],
        out_specs=(WHOLE, WHOLE, WHOLE),
        out_shape=(pltpu.VMEM((NODES, 2 * K, LANES), BF16), *table_and_sent(LEAF_PAIRS)),
        scratch_shapes=[*TRANSPOSE_SCRATCH, pltpu.SemaphoreType.DMA],
        compiler_params=params(12),
    )(in_hbm(slabs), *in_vmem(own, near), in_hbm(next_near))


def upper_table_kernel(own_ref, near_ref, next_ref, table_ref, sent_ref):
    fill_first(own_ref, near_ref, next_ref, table_ref, sent_ref, UPPER_PAIRS)


def upper_table(own, near, next_near):
    return pl.pallas_call(
        upper_table_kernel,
        in_specs=[WHOLE, WHOLE, WHOLE],
        out_specs=(WHOLE, WHOLE),
        out_shape=table_and_sent(UPPER_PAIRS),
        compiler_params=params(4),
    )(*in_vmem(own, near, next_near))


def rest_kernel(leaf_ref, upper_ref, given_leaf, given_upper, leaf_table, upper_table):
    for table, other_ref, pairs in ((leaf_table, leaf_ref, LEAF_PAIRS), (upper_table, upper_ref, UPPER_PAIRS)):
        for step in range(REACH):
            fill_block(table, other_ref, REACH + 1 + step, pairs, step * pairs)


def rest_of_tables(other_leaf, other_upper, leaf_table, table):
    return pl.pallas_call(
        rest_kernel,
        in_specs=[WHOLE] * 4,
        out_specs=(WHOLE, WHOLE),
        out_shape=(table_and_sent(LEAF_PAIRS)[0], table_and_sent(UPPER_PAIRS)[0]),
        input_output_aliases={2: 0, 3: 1},
        compiler_params=params(2),
    )(*in_vmem(other_leaf, other_upper, leaf_table, table))


def couple_pair(j, first_node, place_ref, table, weights_refs):
    low = lax.broadcasted_iota(jnp.int32, (ROWS, LANES), 1) < K

    def fetch(slot, node):
        place = place_ref[slot, node]
        return table[place >> 12, place & 4095]

    products = []
    for side in range(2):
        node = first_node + 2 * j + side
        total = None
        for duo in range(DUOS):
            halves = []
            for half in range(2):
                slot = half * 4 + duo * 2
                halves.append(jnp.where(low, fetch(slot, node), fetch(slot + 1, node)))
            operand = jnp.concatenate(halves, axis=0)
            term = jnp.dot(operand, weights_refs[duo][node], preferred_element_type=F32)
            total = term if total is None else total + term
        products.append(total)
    even, odd = products
    straight = jnp.where(low, even[:ROWS], odd[ROWS:])
    crossed = jnp.where(low, odd[:ROWS], even[ROWS:])
    return straight + swap_halves(crossed)


def leaf_kernel(place_ref, far_ref, first_ref, second_ref, given_ref, out_ref, table):
    fill_block(table, far_ref, 0, LEAF_PAIRS)

    def one(j):
        out_ref[j] = couple_pair(j, 2 * UPPER_PAIRS, place_ref, table, (first_ref, second_ref))

    each(LEAF_PAIRS, LEAF_PAIRS, one)


def leaf_level(place, far, weights, table):
    return pl.pallas_call(
        leaf_kernel,
        in_specs=[IN_SMEM] + [WHOLE] * 4,
        out_specs=(WHOLE, WHOLE),
        out_shape=(pltpu.VMEM((LEAF_PAIRS, ROWS, LANES), F32), table_and_sent(LEAF_PAIRS)[0]),
        input_output_aliases={4: 1},
        compiler_params=params(4),
    )(place, *in_vmem(far, *weights, table))[0]


OUT_PARTS = 4
OUT_STEP = LEAF_PAIRS // 2 // OUT_PARTS


def upper_kernel(place_ref, far_ref, first_ref, second_ref, basis_ref, leaf_ref, given_ref, out_hbm, table, local, out_ref, out_sem):
    fill_block(table, far_ref, 0, UPPER_PAIRS)

    def one(j):
        local[j] = couple_pair(j, 0, place_ref, table, (first_ref, second_ref))

    each(UPPER_PAIRS, UPPER_PAIRS, one)
    def put(part):
        rows = pl.ds(part * 4 * OUT_STEP, 4 * OUT_STEP)
        return pltpu.make_async_copy(out_ref.at[rows], out_hbm.at[rows], out_sem.at[part])

    contract = (((1,), (1,)), ((), ()))
    for level in range(LEV - 1):
        first = pair_offset(level)
        below = pair_offset(level + 1)
        for i in range(2**level):
            parent = local[first + i].astype(BF16)
            children = lax.dot_general(parent, basis_ref[first + i], contract, preferred_element_type=F32)
            for side in range(2):
                part = children[:, side * LANES : (side + 1) * LANES]
                if level == LEV - 2:
                    pair = part + leaf_ref[2 * i + side]
                    out_ref[4 * i + 2 * side] = pair[:, :K]
                    out_ref[4 * i + 2 * side + 1] = swap_halves(pair)[:, :K]
                else:
                    local[below + 2 * i + side] += part
            if level == LEV - 2 and (i + 1) % OUT_STEP == 0:
                put(i // OUT_STEP).start()
    for part in range(OUT_PARTS):
        put(part).wait()


def upper_levels(place, far, weights, basis, leaf, table):
    return pl.pallas_call(
        upper_kernel,
        in_specs=[IN_SMEM] + [WHOLE] * 6,
        out_specs=(IN_HBM, WHOLE),
        out_shape=(
            jax.ShapeDtypeStruct((2 * LEAF_PAIRS, ROWS, K), F32),
            table_and_sent(UPPER_PAIRS)[0],
        ),
        input_output_aliases={6: 1},
        scratch_shapes=[
            pltpu.VMEM((UPPER_PAIRS, ROWS, LANES), F32),
            pltpu.VMEM((2 * LEAF_PAIRS, ROWS, K), F32),
            pltpu.SemaphoreType.DMA((OUT_PARTS,)),
        ],
        compiler_params=params(6),
    )(place, *in_vmem(far, *weights, basis, leaf, table))[0]


def shards(leaf_skel, transfer, tiles, cols):
    count = lax.axis_size("clus")
    own_index = lax.axis_index("clus")

    def moved(block, target):
        return lax.ppermute(block, "clus", [(i, target(i) % count) for i in range(count)])

    def other_core(i):
        return i ^ 1

    def outward(i):
        return i + 2 if i % 2 == 0 else i - 2

    def across(i):
        return i + 1 if i % 2 == 1 else i - 1

    slabs = jnp.transpose(tiles, (1, 2, 3, 0)).reshape(2, SLOTS // 2, K, K, NODES)
    leaf, coeffs = front(leaf_skel, jnp.transpose(transfer, (1, 2, 0)))
    near_leaf, next_leaf = moved(leaf, across), moved(leaf, outward)
    basis, upper = upward(coeffs, leaf)
    near_upper, next_upper = moved(upper, across), moved(upper, outward)
    cols, upper = lax.optimization_barrier((cols, upper))
    first, place = first_weights(slabs, cols, own_index.astype(jnp.int32).reshape(1))
    near_leaf, next_leaf, place = lax.optimization_barrier((near_leaf, next_leaf, place))
    far_leaf = moved(near_leaf, outward)
    second, leaf_table, sent_leaf = second_weights(slabs, leaf, near_leaf, next_leaf)
    other_leaf = moved(sent_leaf, other_core)
    far_upper = moved(near_upper, outward)
    table, sent_upper = upper_table(upper, near_upper, next_upper)
    other_upper = moved(sent_upper, other_core)
    leaf_table, table = rest_of_tables(other_leaf, other_upper, leaf_table, table)
    weights = (first, second)
    leaf_local = leaf_level(place, far_leaf, weights, leaf_table)
    return upper_levels(place, far_upper, weights, basis, leaf_local, table)


def solution(mesh):
    in_specs = (
        P("clus", "rhs", None),
        P("clus", None, None),
        P("clus", None, None, None),
        P("clus", None),
    )
    out_specs = P("clus", "rhs", None)
    return jax.shard_map(shards, mesh=mesh, in_specs=in_specs, out_specs=out_specs, check_vma=False)
```
